128 devices in a mesh: inst: 4 (over z_hi, core), cuts: 32 (over y, x, z_lo).
Axes of the slice: x: 4, y: 4, z: 4 (z_hi: 2, z_lo: 2; z = z_hi * 2 + z_lo), core: 2. Of those that a mesh axis runs over, the one named last changes fastest.
Arguments:
- hidden: bfloat16 [4096, 4096], P(('inst', 'cuts')), may hold values from -6 to 6
- cache_kv: bfloat16 [4096, 128, 1024], P(('inst', 'cuts')), may hold values from -96 to 96
- cache_len: int32 [4096], P(('inst', 'cuts')), may hold values from 1 to 127, as said below
- mig_source: int32 [4096], P(('inst', 'cuts')), may hold values from 0 to 4095, as said below
- expert_ids: int32 [4096, 8], P(('inst', 'cuts')), may hold values from 0 to 127, all different within a row; in each aligned block of 32 rows (0 to 31, 32 to 63, ...) at most 4 rows name the same one
- gate_w: bfloat16 [4096, 8], P(('inst', 'cuts')), may hold values from 0.5 to 2
- attn_gain: bfloat16 [4096], replicated, may hold values from 0.5 to 1.5
- w_query: bfloat16 [4096, 8192], P(None, 'cuts'), may hold values from -0.09375 to 0.09375
- w_keyval: bfloat16 [4096, 1024], P(None, 'cuts'), may hold values from -0.09375 to 0.09375
- q_gain: float32 [128], replicated, may hold values from 0.5 to 8
- k_gain: float32 [128], replicated, may hold values from 0.25 to 1.75
- w_out: bfloat16 [8192, 4096], P('cuts'), may hold values from -0.25 to 0.25
- moe_gain: bfloat16 [4096], replicated, may hold values from 0.099609375 to 1.8984375
- w_gate: bfloat16 [4096, 12288], P(None, 'cuts'), may hold values from -0.09375 to 0.09375
- w_up: bfloat16 [4096, 12288], P(None, 'cuts'), may hold values from -0.09375 to 0.09375
- w_down: bfloat16 [12288, 4096], P('cuts'), may hold values from -0.21875 to 0.21875
Outputs:
- hidden_next: bfloat16 [4096, 4096], P(('inst', 'cuts'))
- cache_next: bfloat16 [4096, 128, 1024], P(('inst', 'cuts'))
The draws below stay inside these ranges and needn't reach their ends.
Inputs may be any that keep to these rules, and one draw needn't show every extreme that they name: `mig_source`: each row is named once. Entry r names either r itself or the row in the same local slot of the device with the same cuts index in another group; each device hands exactly 2 rows to each other group. `cache_len`: rows that come from another group have at least 64 positions.
All inputs are finite; a program needn't handle non-finite values.
Results may differ from the reference program's by a relative error of at most 0.03.
Values may be sent and summed in bfloat16 or wider, within the bound.
No kernel may reach another device: no remote copies, remote signals or barrier semaphores. Data moves between devices by JAX's collectives and lax.ppermute only.
A program may use at most 192 MiB of HBM per device.

```python
import math
import jax
import jax.numpy as jnp
import numpy as np
from jax import lax

D = 4096
QH = 64
KVH = 4
HD = 128
EXPERTS = 128
TOPK = 8
FFW = 768
ROW_DEV = 32
LMAX = 128
MIG = 2
MOST = 4
QL = 2
EXP_WIN = 16
ROWS = 4096
N_INST = 4
N_CUTS = 32


def migration_plan(key):
    key = jax.random.fold_in(key, 37)
    slot_key, shift_key = jax.random.split(key)
    slot_orders = jax.vmap(lambda sub: jax.random.permutation(sub, ROW_DEV))(jax.random.split(slot_key, N_CUTS))
    slot_rank = jnp.argsort(slot_orders, axis=1)
    shift_lists = jax.vmap(lambda sub: jax.random.permutation(sub, N_INST - 1) + 1)(jax.random.split(shift_key, N_CUTS))
    block_index = jnp.minimum(slot_rank // MIG, N_INST - 2)
    leaving = slot_rank < (N_INST - 1) * MIG
    offsets = jnp.where(leaving, jnp.take_along_axis(shift_lists, block_index, axis=1), 0)
    group_index = jnp.arange(N_INST)[:, None, None]
    source_group = (group_index - offsets[None, :, :]) % N_INST
    cut_index = jnp.arange(N_CUTS)[None, :, None]
    slot_index = jnp.arange(ROW_DEV)[None, None, :]
    return ((source_group * N_CUTS + cut_index) * ROW_DEV + slot_index).reshape(-1).astype(jnp.int32)


def draw_cache_kv(key, part):
    key = jax.random.fold_in(key, 11)
    normal_part = jnp.clip(jax.random.normal(key, (ROWS, LMAX, 2 * KVH * HD), jnp.float32), -6.0, 6.0)
    return normal_part.astype(jnp.bfloat16)


def draw_q_gain(key, part):
    key = jax.random.fold_in(key, 17)
    return jax.random.uniform(key, (HD,), jnp.float32, 0.5, 2.0)


def draw_cache_len(key, part):
    sources = migration_plan(key)
    key = jax.random.fold_in(key, 23)
    short_key, long_key, choose_key, place_key = jax.random.split(key, 4)
    short_len = jax.random.randint(short_key, (ROWS,), 1, LMAX // 4 + 1)
    long_len = jax.random.randint(long_key, (ROWS,), LMAX // 2, LMAX)
    is_long = jax.random.randint(choose_key, (ROWS,), 0, 4) == 0
    group_size = ROW_DEV * N_CUTS
    moved = sources // group_size != jnp.arange(ROWS) // group_size
    lengths = jnp.where(is_long | moved, long_len, short_len)
    long_row = jax.random.randint(place_key, (), 0, ROWS)
    lengths = jnp.where(jnp.arange(ROWS) == long_row, LMAX - 1, lengths)
    return lengths.astype(jnp.int32)


def draw_mig_source(key, part):
    return migration_plan(key)


def block_levels(stream_key, extent, cuts, low, high):
    loudness = 1.0
    for axis_at, parts in cuts:
        draws = jax.random.uniform(jax.random.fold_in(jax.random.fold_in(stream_key, 6), axis_at), (parts,), jnp.float32, low / len(cuts), high / len(cuts))
        loudness = loudness * jnp.repeat(jnp.exp(draws), extent[axis_at] // parts).reshape((-1,) + (1,) * (len(extent) - 1 - axis_at))
    return loudness


def assign_block(stream_key, own, number, rows, count, top, reach, slope):
    order = jax.random.permutation(stream_key, count)
    heavy_load, ordinary = shares(count, rows * top, reach, slope, True), shares(count, rows * top, reach, slope, False)
    places = jnp.arange(count)

    def named(sizes, turn):
        used = int((sizes > 0).sum())
        fixed = max(1, used // 4)
        moved = fixed + (places - fixed + turn * (used - fixed)) % max(1, count - fixed)
        return jnp.zeros((count,), jnp.int32).at[order[jnp.where(places < fixed, places, moved)]].set(jnp.asarray(sizes, jnp.int32))

    sizes = jnp.where(number % 4 == 0, named(heavy_load, number // 4), named(ordinary, number - number // 4 - 1))
    mixed = jax.random.permutation(jax.random.fold_in(own, 3), count)
    source_of, taker = mixed[0:count // 2 * 2:2], mixed[1:count // 2 * 2:2]
    room = jnp.minimum(sizes[source_of] - 1, reach - sizes[taker]) // 2
    room = jnp.where((source_of == order[0]) | (taker == order[0]) | (sizes[taker] == 0), 0, jnp.maximum(room, 0))
    moved = jax.random.randint(jax.random.fold_in(own, 4), (count // 2,), 0, 1 << 20) % (room + 1)
    sizes = sizes.at[source_of].add(-moved).at[taker].add(moved)
    items = jnp.searchsorted(jnp.cumsum(sizes), jnp.arange(rows * top), side="right").astype(jnp.int32)
    grid = items.reshape(top, rows).T
    grid = grid[jax.random.permutation(jax.random.fold_in(own, 1), rows)]
    turn = jax.random.randint(jax.random.fold_in(own, 2), (rows, 1), 0, top)
    return jnp.take_along_axis(grid, (jnp.arange(top)[None, :] + turn) % top, axis=1)


def shares(number_of, total, reach, lean, full):
    loads = [(1 << 20) // math.isqrt(grade ** lean) + 1 for grade in range(1, number_of + 1)]
    largest = reach if full else min(reach, max(-(-total // number_of), total * loads[0] // sum(loads)))
    least = 1 if total - largest >= number_of - 1 else 0
    counts, rest = [largest] + [least] * (number_of - 1), total - largest - least * (number_of - 1)
    while rest > 0:
        candidates = [i for i in range(1, number_of) if counts[i] < largest] or [i for i in range(1, number_of) if counts[i] < reach]
        whole, remaining = sum([loads[i] for i in candidates]), rest
        for i in candidates:
            extra = min(reach - counts[i], max(1, remaining * loads[i] // whole), rest)
            counts[i] = counts[i] + extra
            rest = rest - extra
    return np.array(counts)


def centred(own_key, extent, deviation, limit, cuts=(), held_as=jnp.bfloat16):
    result = deviation * jax.random.normal(own_key, extent, jnp.float32)
    if cuts:
        result = result * block_levels(own_key, extent, cuts, -0.22, 0.18)
    return jnp.clip(result, -limit, limit).astype(held_as)


def setup_inputs(seed: int = 0) -> dict:
    streams_of = jax.random.split(jax.random.key(seed), 17)
    hidden = centred(streams_of[0], (ROWS, D), 1.0, 6.0, ((0, 128),))
    cache_kv = draw_cache_kv(jax.random.fold_in(streams_of[16], 71), 0)
    cache_len = draw_cache_len(jax.random.fold_in(streams_of[16], 71), 0)
    mig_source = draw_mig_source(jax.random.fold_in(streams_of[16], 71), 0)
    expert_ids_keys = jax.random.split(jax.random.fold_in(streams_of[4], 1), ROWS // ROW_DEV)
    expert_ids_turns = jax.random.permutation(jax.random.fold_in(streams_of[4], 3), ROWS // ROW_DEV)
    expert_ids = jax.vmap(lambda own, number: assign_block(jax.random.fold_in(streams_of[4], 2), own, number, ROW_DEV, EXPERTS, TOPK, MOST, 2))(expert_ids_keys, expert_ids_turns).reshape((ROWS, TOPK))
    gate_w = jnp.clip(0.5 + 1.5 * jax.random.uniform(streams_of[5], (ROWS, TOPK), jnp.float32) ** block_levels(streams_of[5], (ROWS, TOPK), ((0, 128),), -0.2, 0.2), 0.5, 2.0).astype(jnp.bfloat16)
    attn_gain = jnp.clip(1.0 + 0.1 * jax.random.normal(streams_of[6], (D,), jnp.float32), 0.5, 1.5).astype(jnp.bfloat16)
    w_query = centred(streams_of[7], (D, QH * HD), D ** -0.5, 0.09375, ((1, 32),))
    w_keyval = centred(streams_of[8], (D, 2 * KVH * HD), D ** -0.5, 0.09375, ((1, 32),))
    q_gain = draw_q_gain(jax.random.fold_in(streams_of[16], 71), 0)
    k_gain = jnp.clip(1.0 + 0.15 * jax.random.normal(streams_of[10], (HD,), jnp.float32), 0.25, 1.75)
    w_out = centred(streams_of[11], (QH * HD, D), (4 * HD) ** -0.5, 0.25, ((0, 32),))
    moe_gain = jnp.clip(1.0 + 0.18 * jax.random.normal(streams_of[12], (D,), jnp.float32), 0.099609375, 1.8984375).astype(jnp.bfloat16)
    w_gate = centred(streams_of[13], (D, EXP_WIN * FFW), D ** -0.5, 0.09375, ((1, 32),))
    w_up = centred(streams_of[14], (D, EXP_WIN * FFW), D ** -0.5, 0.09375, ((1, 32),))
    w_down = centred(streams_of[15], (EXP_WIN * FFW, D), FFW ** -0.5, 0.21875, ((0, 32),))
    return dict(hidden=hidden, cache_kv=cache_kv, cache_len=cache_len, mig_source=mig_source, expert_ids=expert_ids, gate_w=gate_w, attn_gain=attn_gain, w_query=w_query, w_keyval=w_keyval, q_gain=q_gain, k_gain=k_gain, w_out=w_out, moe_gain=moe_gain, w_gate=w_gate, w_up=w_up, w_down=w_down)


EPSILON = 1e-06
ROPE_BASE = 1000000.0

def norm_rows(values, gain_vec):
    mean_square = lax.optimization_barrier(jnp.mean(values * values, axis=-1, keepdims=True))
    return values * lax.rsqrt(mean_square + EPSILON) * gain_vec

def rotate(values, position):
    half_width = values.shape[-1] // 2
    frequency = ROPE_BASE ** (-2.0 * jnp.arange(half_width, dtype=jnp.float32) / values.shape[-1])
    angles = position.astype(jnp.float32)[:, None] * frequency[None, :]
    cosine = jnp.concatenate([jnp.cos(angles), jnp.cos(angles)], axis=-1)[:, None, :]
    sine_part = jnp.concatenate([jnp.sin(angles), jnp.sin(angles)], axis=-1)[:, None, :]
    turned = jnp.concatenate([-values[..., half_width:], values[..., :half_width]], axis=-1)
    return values * cosine + turned * sine_part

def attend(q_raw, kv_raw, cache_rows, lengths, q_gain, k_gain):
    row_count = q_raw.shape[0]
    head_count = q_raw.shape[1] // HD
    kv_count = kv_raw.shape[1] // (2 * HD)
    group_size = head_count // kv_count
    length_cap = cache_rows.shape[1]
    queries = norm_rows(q_raw.astype(jnp.float32).reshape(row_count, head_count, HD), q_gain.astype(jnp.float32))
    queries = rotate(queries, lengths).astype(jnp.bfloat16).reshape(row_count, kv_count, group_size, HD)
    key_raw = kv_raw[:, :kv_count * HD].astype(jnp.float32).reshape(row_count, kv_count, HD)
    key_new = rotate(norm_rows(key_raw, k_gain.astype(jnp.float32)), lengths).astype(jnp.bfloat16)
    value_new = kv_raw[:, kv_count * HD:].reshape(row_count, kv_count, HD)
    key_cache = cache_rows[:, :, :kv_count * HD].reshape(row_count, length_cap, kv_count, HD)
    value_cache = cache_rows[:, :, kv_count * HD:].reshape(row_count, length_cap, kv_count, HD)
    score_scale = HD ** (-0.5)
    scores = jnp.einsum('rkgd,rpkd->rkgp', queries.astype(jnp.float32), key_cache.astype(jnp.float32)) * score_scale
    positions = jnp.arange(length_cap, dtype=jnp.int32)
    usable = positions[None, :] < lengths[:, None]
    scores = jnp.where(usable[:, None, None, :], scores, -jnp.inf)
    self_score = jnp.einsum('rkgd,rkd->rkg', queries.astype(jnp.float32), key_new.astype(jnp.float32)) * score_scale
    peak = jnp.maximum(lax.optimization_barrier(jnp.max(scores, axis=-1)), self_score)
    weights = jnp.exp(scores - peak[..., None])
    self_weight = jnp.exp(self_score - peak)
    denominator = lax.optimization_barrier(jnp.sum(weights, axis=-1)) + self_weight
    probs = (weights / denominator[..., None]).astype(jnp.bfloat16)
    self_prob = (self_weight / denominator).astype(jnp.bfloat16)
    summed = jnp.einsum('rkgp,rpkd->rkgd', probs.astype(jnp.float32), value_cache.astype(jnp.float32))
    summed = summed + self_prob.astype(jnp.float32)[..., None] * value_new.astype(jnp.float32)[:, :, None, :]
    attention = summed.reshape(row_count, head_count * HD).astype(jnp.bfloat16)
    new_entry = jnp.concatenate([key_new.reshape(row_count, -1), value_new.reshape(row_count, -1)], axis=-1)
    at_length = (positions[None, :] == lengths[:, None])[:, :, None]
    cache_next = jnp.where(at_length, new_entry[:, None, :], cache_rows)
    return (attention, cache_next)

def reference(hidden, cache_kv, cache_len, mig_source, expert_ids, gate_w, attn_gain, w_query, w_keyval, q_gain, k_gain, w_out, moe_gain, w_gate, w_up, w_down):
    migrated = jnp.take(hidden, mig_source, axis=0)
    cache_rows = jnp.take(cache_kv, mig_source, axis=0)
    row_count = hidden.shape[0]
    normed = norm_rows(migrated.astype(jnp.float32), attn_gain.astype(jnp.float32)).astype(jnp.bfloat16)
    q_raw = jnp.dot(normed, w_query, preferred_element_type=jnp.float32).astype(jnp.bfloat16)
    kv_raw = jnp.dot(normed, w_keyval, preferred_element_type=jnp.float32).astype(jnp.bfloat16)
    group_rows = row_count // N_INST

    def per_group(items):
        return attend(items[0], items[1], items[2], items[3], q_gain, k_gain)
    attention, cache_next = lax.map(per_group, (q_raw.reshape(N_INST, group_rows, -1), kv_raw.reshape(N_INST, group_rows, -1), cache_rows.reshape(N_INST, group_rows, LMAX, -1), cache_len.reshape(N_INST, group_rows)))
    attention = attention.reshape(row_count, -1)
    cache_next = cache_next.reshape(cache_kv.shape)
    block_width = QL * HD

    def out_step(block_id, running):
        slab_rows = lax.dynamic_slice_in_dim(attention, block_id * block_width, block_width, 1)
        weight = lax.dynamic_slice_in_dim(w_out, block_id * block_width, block_width, 0)
        partial_value = jnp.dot(slab_rows, weight, preferred_element_type=jnp.float32).astype(jnp.bfloat16)
        partial_value = lax.optimization_barrier(partial_value)
        return running + partial_value.astype(jnp.float32)
    attn_out = lax.fori_loop(0, N_CUTS, out_step, jnp.zeros((row_count, D), jnp.float32))
    mixed_rows = migrated.astype(jnp.float32) + attn_out
    moe_rows = norm_rows(mixed_rows, moe_gain.astype(jnp.float32)).astype(jnp.bfloat16)
    expert_range = jnp.arange(EXP_WIN, dtype=jnp.int32)
    combine = lax.optimization_barrier(jnp.sum(jnp.where(expert_ids[:, :, None] == expert_range[None, None, :], gate_w.astype(jnp.float32)[:, :, None], jnp.zeros((), jnp.float32)), axis=1))
    half_width = FFW // 2

    def expert_step(block_id, running):
        weight_gate = lax.dynamic_slice_in_dim(w_gate, block_id * half_width, half_width, 1)
        weight_up = lax.dynamic_slice_in_dim(w_up, block_id * half_width, half_width, 1)
        weight_down = lax.dynamic_slice_in_dim(w_down, block_id * half_width, half_width, 0)
        scale_column = lax.dynamic_slice_in_dim(combine, block_id // 2, 1, 1)
        gate_part = jnp.dot(moe_rows, weight_gate, preferred_element_type=jnp.float32)
        upward = jnp.dot(moe_rows, weight_up, preferred_element_type=jnp.float32)
        activation = (jax.nn.silu(gate_part) * upward * scale_column).astype(jnp.bfloat16)
        partial_value = jnp.dot(activation, weight_down, preferred_element_type=jnp.float32).astype(jnp.bfloat16)
        partial_value = lax.optimization_barrier(partial_value)
        return running + partial_value.astype(jnp.float32)
    moe_out = lax.fori_loop(0, N_CUTS, expert_step, jnp.zeros((row_count, D), jnp.float32))
    hidden_next = (mixed_rows + moe_out).astype(jnp.bfloat16)
    return (hidden_next, cache_next)
```

```python
import functools
import jax
import jax.numpy as jnp
from jax import lax
from jax.experimental import pallas as pl
from jax.experimental.pallas import tpu as pltpu
from jax.sharding import PartitionSpec as P

HD = 128
MIG = 2
MOST = 4
EPSILON = 1e-06
ROPE_BASE = 1000000.0
SIDE = 4
PLANE = SIDE * SIDE
BF16 = jnp.bfloat16
F32 = jnp.float32


def cut_index(y, x, z):
    return (y * SIDE + x) * 2 + z


PLANES = [[cut_index(y, x, z) for y in range(SIDE) for x in range(SIDE)] for z in range(2)]


def pair_perm(side):
    out = []
    for z in range(4):
        other = z ^ 1 if side == 0 else (z + 1 if z % 2 else z - 1) % 4
        for core in range(2):
            for y in range(SIDE):
                for x in range(SIDE):
                    out.append(
                        (
                            ((z // 2) * 2 + core) * 32 + cut_index(y, x, z % 2),
                            ((other // 2) * 2 + core) * 32 + cut_index(y, x, other % 2),
                        )
                    )
    return out


def from_pair(array, side):
    return lax.ppermute(array, ("inst", "cuts"), pair_perm(side))


def norm_rows(values, gain_vec):
    mean_square = jnp.mean(values * values, axis=-1, keepdims=True)
    return values * lax.rsqrt(mean_square + EPSILON) * gain_vec


def attend_kernel(
    lens_ref, q_ref, kv_ref, cos_ref, sin_ref, qg_ref, kg_ref, cache_ref,
    att_ref, entry_ref, qs_ref, ks_ref, vs_ref, os_ref, *, rows_step, kv_count, group_size,
):
    step = pl.program_id(0)
    peers = q_ref.shape[0]
    per_peer = att_ref.shape[2] // HD
    length_cap = cache_ref.shape[1]
    width = kv_count * HD

    @pl.when(step == 0)
    def _():
        cosine = cos_ref[...]
        sine = sin_ref[...]

        def prepare(values, gain):
            values = norm_rows(values, gain)
            return values * cosine + pltpu.roll(values, HD // 2, 1) * sine

        for p in range(peers):
            for j in range(per_peer):
                values = q_ref[p, :, j * HD : (j + 1) * HD].astype(F32)
                qs_ref[:, p * per_peer + j, :] = prepare(values, qg_ref[...])
        for k in range(kv_count):
            key = prepare(kv_ref[:, k * HD : (k + 1) * HD].astype(F32), kg_ref[...]).astype(BF16)
            entry_ref[:, k * HD : (k + 1) * HD] = key
            ks_ref[:, k, :] = key.astype(F32)
            value = kv_ref[:, width + k * HD : width + (k + 1) * HD]
            entry_ref[:, width + k * HD : width + (k + 1) * HD] = value
            vs_ref[:, k, :] = value.astype(F32)

    scale = HD ** (-0.5)
    heads = kv_count * group_size
    positions = lax.broadcasted_iota(jnp.int32, (heads, length_cap), 1)
    spans = [slice(k * group_size, (k + 1) * group_size) for k in range(kv_count)]
    first = step * rows_step
    queries = [qs_ref[first + i].astype(BF16) for i in range(rows_step)]
    keys_new = [ks_ref[first + i] for i in range(rows_step)]
    values_new = [vs_ref[first + i] for i in range(rows_step)]
    scores = [
        jnp.concatenate(
            [
                lax.dot_general(
                    queries[i][spans[k]], cache_ref[i, :, k * HD : (k + 1) * HD],
                    (((1,), (1,)), ((), ())), preferred_element_type=F32,
                )
                for k in range(kv_count)
            ],
            axis=0,
        )
        for i in range(rows_step)
    ]
    outs = []
    for i in range(rows_step):
        spread = jnp.concatenate(
            [
                jnp.broadcast_to(keys_new[i][k : k + 1], (group_size, HD))
                for k in range(kv_count)
            ],
            axis=0,
        )
        self_score = jnp.sum(queries[i].astype(F32) * spread, axis=1, keepdims=True) * scale
        score = jnp.where(positions < lens_ref[first + i], scores[i] * scale, -1e30)
        peak = jnp.maximum(jnp.max(score, axis=1, keepdims=True), self_score)
        weights = jnp.exp(score - peak)
        self_weight = jnp.exp(self_score - peak)
        inverse = 1.0 / (jnp.sum(weights, axis=1, keepdims=True) + self_weight)
        outs.append(
            ((weights * inverse).astype(BF16), (self_weight * inverse).astype(BF16).astype(F32))
        )
    results = [
        jnp.concatenate(
            [
                jnp.dot(
                    outs[i][0][spans[k]],
                    cache_ref[i, :, width + k * HD : width + (k + 1) * HD],
                    preferred_element_type=F32,
                )
                + outs[i][1][spans[k]] * values_new[i][k : k + 1]
                for k in range(kv_count)
            ],
            axis=0,
        )
        for i in range(rows_step)
    ]
    for i in range(rows_step):
        os_ref[first + i] = results[i]

    @pl.when(step == pl.num_programs(0) - 1)
    def _():
        for p in range(peers):
            for j in range(per_peer):
                att_ref[p, :, j * HD : (j + 1) * HD] = os_ref[:, p * per_peer + j, :].astype(BF16)


def attend(q_peers, q_width, kv_rows, cache_kv, lengths, q_gain, k_gain):
    peers, rows, sent_width = q_peers.shape
    length_cap, entry_width = cache_kv.shape[1:]
    kv_count = entry_width // (2 * HD)
    heads = peers * q_width // HD
    rows_step = 4
    frequency = ROPE_BASE ** (-2.0 * jnp.arange(HD // 2, dtype=F32) / HD)
    angles = lengths.astype(F32)[:, None] * frequency[None, :]
    cosine = jnp.concatenate([jnp.cos(angles), jnp.cos(angles)], axis=-1)
    sine = jnp.concatenate([-jnp.sin(angles), jnp.sin(angles)], axis=-1)
    whole = lambda shape: pl.BlockSpec(shape, lambda i, lens: (0,) * len(shape))
    return pl.pallas_call(
        functools.partial(
            attend_kernel, rows_step=rows_step, kv_count=kv_count, group_size=heads // kv_count
        ),
        grid_spec=pltpu.PrefetchScalarGridSpec(
            num_scalar_prefetch=1,
            grid=(rows // rows_step,),
            in_specs=[
                whole((peers, rows, sent_width)),
                whole((rows, entry_width)),
                whole((rows, HD)),
                whole((rows, HD)),
                whole((1, HD)),
                whole((1, HD)),
                pl.BlockSpec((rows_step, length_cap, entry_width), lambda i, lens: (i, 0, 0)),
            ],
            out_specs=[whole((peers, rows, q_width)), whole((rows, entry_width))],
            scratch_shapes=[
                pltpu.VMEM((rows, heads, HD), F32),
                pltpu.VMEM((rows, kv_count, HD), F32),
                pltpu.VMEM((rows, kv_count, HD), F32),
                pltpu.VMEM((rows, heads, HD), F32),
            ],
        ),
        out_shape=[
            jax.ShapeDtypeStruct((peers, rows, q_width), BF16),
            jax.ShapeDtypeStruct((rows, entry_width), BF16),
        ],
        compiler_params=pltpu.CompilerParams(vmem_limit_bytes=32 * 1024 * 1024),
        cost_estimate=pl.CostEstimate(
            flops=4 * rows * heads * HD * length_cap,
            bytes_accessed=cache_kv.size * 2 + q_peers.size * 4,
            transcendentals=rows * heads * length_cap,
        ),
        name="attend",
    )(lengths, q_peers, kv_rows, cosine, sine, q_gain[None, :], k_gain[None, :], cache_kv)


def place_kernel(lens_ref, arrive_ref, slot_ref, entry_ref, cache_ref, landed_ref, out_ref):
    row = pl.program_id(0)
    position = lax.broadcasted_iota(jnp.int32, out_ref.shape[1:], 0)
    at_length = position == lens_ref[row]

    @pl.when(arrive_ref[row] == 0)
    def _():
        out_ref[0] = jnp.where(at_length, entry_ref[0], cache_ref[0])

    @pl.when(arrive_ref[row] != 0)
    def _():
        out_ref[0] = jnp.where(at_length, entry_ref[0], landed_ref[0])


def place_cache(lengths, arriving, landed_slot, entries, cache_kv, landed):
    rows, length_cap, entry_width = cache_kv.shape
    return pl.pallas_call(
        place_kernel,
        grid_spec=pltpu.PrefetchScalarGridSpec(
            num_scalar_prefetch=3,
            grid=(rows,),
            in_specs=[
                pl.BlockSpec((1, 1, entry_width), lambda i, a, b, c: (i, 0, 0)),
                pl.BlockSpec((1, length_cap, entry_width), lambda i, a, b, c: (i, 0, 0)),
                pl.BlockSpec((1, length_cap, entry_width), lambda i, a, b, c: (c[i], 0, 0)),
            ],
            out_specs=pl.BlockSpec((1, length_cap, entry_width), lambda i, a, b, c: (i, 0, 0)),
        ),
        out_shape=jax.ShapeDtypeStruct(cache_kv.shape, BF16),
        compiler_params=pltpu.CompilerParams(vmem_limit_bytes=16 * 1024 * 1024),
        cost_estimate=pl.CostEstimate(
            flops=0, bytes_accessed=cache_kv.size * 4, transcendentals=0
        ),
        name="place_cache",
    )(lengths, arriving.astype(jnp.int32), landed_slot, entries[:, None, :], cache_kv, landed)


def pick_kernel(slot_ref, *refs):
    count = len(refs) // 2
    for source, target in zip(refs[:count], refs[count:]):
        target[...] = source[...]


def pick_caches(slots, cache_kv):
    shifts, count = slots.shape
    block = (1,) + cache_kv.shape[1:]
    return pl.pallas_call(
        pick_kernel,
        grid_spec=pltpu.PrefetchScalarGridSpec(
            num_scalar_prefetch=1,
            grid=(count,),
            in_specs=[
                pl.BlockSpec(block, lambda i, slots, k=k: (slots[k, i], 0, 0))
                for k in range(shifts)
            ],
            out_specs=[pl.BlockSpec(block, lambda i, slots: (i, 0, 0)) for k in range(shifts)],
        ),
        out_shape=[
            jax.ShapeDtypeStruct((count,) + cache_kv.shape[1:], BF16) for k in range(shifts)
        ],
        compiler_params=pltpu.CompilerParams(vmem_limit_bytes=16 * 1024 * 1024),
        cost_estimate=pl.CostEstimate(
            flops=0,
            bytes_accessed=4 * shifts * count * cache_kv.shape[1] * cache_kv.shape[2],
            transcendentals=0,
        ),
        name="pick_caches",
    )(slots, *([cache_kv] * shifts))


def exchange(array):
    return lax.all_to_all(array, "cuts", 0, 0, tiled=True, axis_index_groups=PLANES)


def body(
    hidden,
    cache_kv,
    cache_len,
    mig_source,
    expert_ids,
    gate_w,
    attn_gain,
    w_query,
    w_keyval,
    q_gain,
    k_gain,
    w_out,
    moe_gain,
    w_gate,
    w_up,
    w_down,
):
    group_count = lax.axis_size("inst")
    cut_count = lax.axis_size("cuts")
    local_rows, width = hidden.shape
    group_total = local_rows * cut_count
    group_id = lax.axis_index("inst")
    cut_id = lax.axis_index("cuts")
    low = cut_id % 2 == 0
    slot_ids = jnp.arange(local_rows, dtype=jnp.int32)
    own_rows = (group_id * cut_count + cut_id) * local_rows + slot_ids

    w_query_pair = from_pair(w_query, 0)
    w_keyval_pair = from_pair(w_keyval, 0)
    w_out_pair = from_pair(w_out, 1)

    normed = norm_rows(hidden.astype(F32), attn_gain.astype(F32)).astype(BF16)
    plane_rows = exchange(jnp.broadcast_to(normed[None], (PLANE,) + normed.shape)).reshape(
        PLANE * local_rows, width
    )

    facts = jnp.stack([mig_source, cache_len]).astype(F32)
    all_facts = lax.all_to_all(
        jnp.broadcast_to(facts[None], (group_count,) + facts.shape), "inst", 0, 0, tiled=True
    )
    goes_to = all_facts[:, 0].astype(jnp.int32) == own_rows[None, :]
    lengths = jnp.sum(jnp.where(goes_to, all_facts[:, 1], 0.0), axis=0).astype(jnp.int32)
    targets = jnp.arange(group_count, dtype=jnp.int32)
    leaving = goes_to & (targets[:, None] != group_id)
    leave_rank = jnp.cumsum(leaving.astype(jnp.int32), axis=1) - 1
    chosen = leaving[:, None, :] & (
        leave_rank[:, None, :] == jnp.arange(MIG, dtype=jnp.int32)[None, :, None]
    )
    send_slot = jnp.sum(jnp.where(chosen, slot_ids[None, None, :], 0), axis=2)
    source_group = mig_source // group_total
    arriving = source_group != group_id
    from_group = (source_group[None, :] == targets[:, None]) & arriving[None, :]
    arrival_rank = jnp.sum(
        jnp.where(from_group, jnp.cumsum(from_group.astype(jnp.int32), axis=1) - 1, 0), axis=0
    )
    source_pick = jnp.where(arriving, source_group, 0)

    shifts = jnp.arange(1, group_count, dtype=jnp.int32)
    picked = pick_caches(send_slot[(group_id + shifts) % group_count], cache_kv)
    landed = jnp.concatenate(
        [
            lax.ppermute(
                array, "inst", [(g, (g + shift) % group_count) for g in range(group_count)]
            )
            for shift, array in zip(range(1, group_count), picked)
        ]
    )
    distance = (group_id - source_group) % group_count
    landed_slot = jnp.where(arriving, (distance - 1) * MIG + arrival_rank, 0)

    w_project = jnp.concatenate([w_query, w_query_pair, w_keyval, w_keyval_pair], axis=1)
    projected = jnp.dot(plane_rows, w_project, preferred_element_type=F32).astype(BF16)
    arrived = exchange(projected.reshape(PLANE, local_rows, -1))
    q_width = 2 * w_query.shape[1]
    kv_width = w_keyval.shape[1]
    own_kv = arrived[:, :, q_width : q_width + kv_width]
    pair_kv = arrived[:, :, q_width + kv_width :]
    kv_rows = jnp.where(
        low,
        jnp.concatenate([own_kv, pair_kv], axis=2),
        jnp.concatenate([pair_kv, own_kv], axis=2),
    )
    kv_rows = jnp.transpose(kv_rows, (1, 0, 2)).reshape(local_rows, -1)
    attention, entries = attend(arrived, q_width, kv_rows, cache_kv, lengths, q_gain, k_gain)

    w_gate, w_up, w_down, arrived_mark = lax.optimization_barrier(
        (w_gate, w_up, w_down, w_project)
    )
    w_gate_pair = from_pair(w_gate, 0)
    w_up_pair = from_pair(w_up, 1)

    w_out_both = jnp.concatenate([w_out, w_out_pair])
    attn_heads = exchange(attention).reshape(PLANE * local_rows, q_width)
    attn_heads, w_gate_pair, w_up_pair, landed, w_down = lax.optimization_barrier(
        (attn_heads, w_gate_pair, w_up_pair, landed, w_down)
    )
    w_down_pair = from_pair(w_down, 0)
    partial_value = jnp.dot(attn_heads, w_out_both, preferred_element_type=F32).astype(BF16)
    sums = exchange(partial_value.reshape(PLANE, local_rows, width))

    got_entries = lax.all_to_all(entries[send_slot], "inst", 0, 0, tiled=True)
    new_entries = jnp.where(arriving[:, None], got_entries[source_pick, arrival_rank], entries)
    cache_next = place_cache(cache_len, arriving, landed_slot, new_entries, cache_kv, landed)
    sums, cache_next, w_down_pair = lax.optimization_barrier((sums, cache_next, w_down_pair))

    mixed_rows = hidden.astype(F32) + jnp.sum(sums.astype(F32), axis=0)
    got_rows = lax.all_to_all(mixed_rows[send_slot], "inst", 0, 0, tiled=True)
    mixed_rows = jnp.where(arriving[:, None], got_rows[source_pick, arrival_rank], mixed_rows)
    moe_local = norm_rows(mixed_rows, moe_gain.astype(F32)).astype(BF16)

    expert_range = jnp.arange(PLANE, dtype=jnp.int32)
    combine = jnp.sum(
        jnp.where(
            expert_ids[:, :, None] == expert_range[None, None, :],
            gate_w.astype(F32)[:, :, None],
            0.0,
        ),
        axis=1,
    )
    flags = jnp.transpose(combine) > 0.0
    rank = jnp.cumsum(flags.astype(jnp.int32), axis=1) - 1
    slot_range = jnp.arange(MOST, dtype=jnp.int32)
    match = flags[:, None, :] & (rank[:, None, :] == slot_range[None, :, None])
    match = match.reshape(PLANE * MOST, local_rows)
    slab = jnp.dot(match.astype(BF16), moe_local, preferred_element_type=F32).astype(BF16)
    slab_rows = exchange(slab.reshape(PLANE, MOST, width)).reshape(PLANE * MOST, width)

    def expert_half(gate, up, down):
        gate_part = jnp.dot(slab_rows, gate, preferred_element_type=F32)
        upward = jnp.dot(slab_rows, up, preferred_element_type=F32)
        activation = (jax.nn.silu(gate_part) * upward).astype(BF16)
        return jnp.dot(activation, down, preferred_element_type=F32)

    expert_out = (
        expert_half(w_gate, w_up, w_down) + expert_half(w_gate_pair, w_up_pair, w_down_pair)
    ).astype(BF16)
    returned = exchange(expert_out.reshape(PLANE, MOST, width)).reshape(PLANE * MOST, width)
    slot_gate = jnp.where(
        match, jnp.repeat(jnp.transpose(combine), MOST, axis=0), 0.0
    ).astype(BF16)
    moe_out = lax.dot_general(
        slot_gate, returned, (((0,), (0,)), ((), ())), preferred_element_type=F32
    )
    hidden_next = (mixed_rows + moe_out).astype(BF16)
    return (hidden_next, cache_next)


def solution(mesh):
    in_specs = (
        P(("inst", "cuts"), None),
        P(("inst", "cuts"), None, None),
        P(("inst", "cuts")),
        P(("inst", "cuts")),
        P(("inst", "cuts"), None),
        P(("inst", "cuts"), None),
        P(),
        P(None, "cuts"),
        P(None, "cuts"),
        P(),
        P(),
        P("cuts", None),
        P(),
        P(None, "cuts"),
        P(None, "cuts"),
        P("cuts", None),
    )
    out_specs = (P(("inst", "cuts"), None), P(("inst", "cuts"), None, None))
    return jax.shard_map(body, mesh=mesh, in_specs=in_specs, out_specs=out_specs, check_vma=False)
```

```python
import functools
import jax
import jax.numpy as jnp
from jax import lax
from jax.experimental import pallas as pl
from jax.experimental.pallas import tpu as pltpu
from jax.sharding import PartitionSpec as P

HD = 128
MIG = 2
MOST = 4
EPSILON = 1e-06
ROPE_BASE = 1000000.0
SIDE = 4
PLANE = SIDE * SIDE
VMEM_BYTES = 56 * 1024 * 1024
BF16 = jnp.bfloat16
F32 = jnp.float32


def cut_index(y, x, z):
    return (y * SIDE + x) * 2 + z


PLANES = [[cut_index(y, x, z) for y in range(SIDE) for x in range(SIDE)] for z in range(2)]
COLUMNS = [[cut_index(y, x, z) for y in range(SIDE)] for x in range(SIDE) for z in range(2)]


def shift(array, dy, dx):
    moves = [
        (cut_index(y, x, z), cut_index((y + dy) % SIDE, (x + dx) % SIDE, z))
        for y in range(SIDE)
        for x in range(SIDE)
        for z in range(2)
    ]
    return lax.ppermute(array, "cuts", moves)


def pair_perm(side):
    out = []
    for z in range(4):
        other = z ^ 1 if side == 0 else (z + 1 if z % 2 else z - 1) % 4
        for core in range(2):
            for y in range(SIDE):
                for x in range(SIDE):
                    out.append(
                        (
                            ((z // 2) * 2 + core) * 32 + cut_index(y, x, z % 2),
                            ((other // 2) * 2 + core) * 32 + cut_index(y, x, other % 2),
                        )
                    )
    return out


def from_pair(array, side):
    return lax.ppermute(array, ("inst", "cuts"), pair_perm(side))


def norm_rows(values, gain_vec):
    mean_square = jnp.mean(values * values, axis=-1, keepdims=True)
    return values * lax.rsqrt(mean_square + EPSILON) * gain_vec


def attend_kernel(
    lens_ref, q_ref, kv_ref, cos_ref, sin_ref, qg_ref, kg_ref, cache_ref,
    att_ref, entry_ref, qs_ref, ks_ref, vs_ref, os_ref, *, rows_step, kv_count, group_size,
):
    step = pl.program_id(0)
    peers = q_ref.shape[0]
    per_peer = att_ref.shape[2] // HD
    length_cap = cache_ref.shape[1]
    width = kv_count * HD

    @pl.when(step == 0)
    def _():
        cosine = cos_ref[...]
        sine = sin_ref[...]

        def prepare(values, gain):
            values = norm_rows(values, gain)
            return values * cosine + pltpu.roll(values, HD // 2, 1) * sine

        for p in range(peers):
            for j in range(per_peer):
                values = q_ref[p, :, j * HD : (j + 1) * HD].astype(F32)
                qs_ref[:, p * per_peer + j, :] = prepare(values, qg_ref[...])
        for k in range(kv_count):
            key = prepare(kv_ref[:, k * HD : (k + 1) * HD].astype(F32), kg_ref[...]).astype(BF16)
            entry_ref[:, k * HD : (k + 1) * HD] = key
            ks_ref[:, k, :] = key.astype(F32)
            value = kv_ref[:, width + k * HD : width + (k + 1) * HD]
            entry_ref[:, width + k * HD : width + (k + 1) * HD] = value
            vs_ref[:, k, :] = value.astype(F32)

    scale = HD ** (-0.5)
    heads = kv_count * group_size
    positions = lax.broadcasted_iota(jnp.int32, (heads, length_cap), 1)
    spans = [slice(k * group_size, (k + 1) * group_size) for k in range(kv_count)]
    first = step * rows_step
    queries = [qs_ref[first + i].astype(BF16) for i in range(rows_step)]
    keys_new = [ks_ref[first + i] for i in range(rows_step)]
    values_new = [vs_ref[first + i] for i in range(rows_step)]
    scores = [
        jnp.concatenate(
            [
                lax.dot_general(
                    queries[i][spans[k]], cache_ref[i, :, k * HD : (k + 1) * HD],
                    (((1,), (1,)), ((), ())), preferred_element_type=F32,
                )
                for k in range(kv_count)
            ],
            axis=0,
        )
        for i in range(rows_step)
    ]
    outs = []
    for i in range(rows_step):
        spread = jnp.concatenate(
            [
                jnp.broadcast_to(keys_new[i][k : k + 1], (group_size, HD))
                for k in range(kv_count)
            ],
            axis=0,
        )
        self_score = jnp.sum(queries[i].astype(F32) * spread, axis=1, keepdims=True) * scale
        score = jnp.where(positions < lens_ref[first + i], scores[i] * scale, -1e30)
        peak = jnp.maximum(jnp.max(score, axis=1, keepdims=True), self_score)
        weights = jnp.exp(score - peak)
        self_weight = jnp.exp(self_score - peak)
        inverse = 1.0 / (jnp.sum(weights, axis=1, keepdims=True) + self_weight)
        outs.append(
            ((weights * inverse).astype(BF16), (self_weight * inverse).astype(BF16).astype(F32))
        )
    results = [
        jnp.concatenate(
            [
                jnp.dot(
                    outs[i][0][spans[k]],
                    cache_ref[i, :, width + k * HD : width + (k + 1) * HD],
                    preferred_element_type=F32,
                )
                + outs[i][1][spans[k]] * values_new[i][k : k + 1]
                for k in range(kv_count)
            ],
            axis=0,
        )
        for i in range(rows_step)
    ]
    for i in range(rows_step):
        os_ref[first + i] = results[i]

    @pl.when(step == pl.num_programs(0) - 1)
    def _():
        for p in range(peers):
            for j in range(per_peer):
                att_ref[p, :, j * HD : (j + 1) * HD] = os_ref[:, p * per_peer + j, :].astype(BF16)


def attend(q_peers, q_width, kv_rows, cache_kv, first_row, lengths, q_gain, k_gain):
    peers, rows, sent_width = q_peers.shape
    length_cap, entry_width = cache_kv.shape[1:]
    kv_count = entry_width // (2 * HD)
    heads = peers * q_width // HD
    rows_step = 4
    first_step = first_row // rows_step
    frequency = ROPE_BASE ** (-2.0 * jnp.arange(HD // 2, dtype=F32) / HD)
    angles = lengths.astype(F32)[:, None] * frequency[None, :]
    cosine = jnp.concatenate([jnp.cos(angles), jnp.cos(angles)], axis=-1)
    sine = jnp.concatenate([-jnp.sin(angles), jnp.sin(angles)], axis=-1)
    whole = lambda shape: pl.BlockSpec(shape, lambda i, lens: (0,) * len(shape))
    return pl.pallas_call(
        functools.partial(
            attend_kernel, rows_step=rows_step, kv_count=kv_count, group_size=heads // kv_count
        ),
        grid_spec=pltpu.PrefetchScalarGridSpec(
            num_scalar_prefetch=1,
            grid=(rows // rows_step,),
            in_specs=[
                whole((peers, rows, sent_width)),
                whole((rows, entry_width)),
                whole((rows, HD)),
                whole((rows, HD)),
                whole((1, HD)),
                whole((1, HD)),
                pl.BlockSpec((rows_step, length_cap, entry_width), lambda i, lens: (i + first_step, 0, 0)),
            ],
            out_specs=[whole((peers, rows, q_width)), whole((rows, entry_width))],
            scratch_shapes=[
                pltpu.VMEM((rows, heads, HD), F32),
                pltpu.VMEM((rows, kv_count, HD), F32),
                pltpu.VMEM((rows, kv_count, HD), F32),
                pltpu.VMEM((rows, heads, HD), F32),
            ],
        ),
        out_shape=[
            jax.ShapeDtypeStruct((peers, rows, q_width), BF16),
            jax.ShapeDtypeStruct((rows, entry_width), BF16),
        ],
        compiler_params=pltpu.CompilerParams(vmem_limit_bytes=VMEM_BYTES),
        cost_estimate=pl.CostEstimate(
            flops=4 * rows * heads * HD * length_cap,
            bytes_accessed=rows * length_cap * entry_width * 2 + q_peers.size * 4,
            transcendentals=rows * heads * length_cap,
        ),
        name="attend",
    )(lengths, q_peers, kv_rows, cosine, sine, q_gain[None, :], k_gain[None, :], cache_kv)


WINDOW = 16


def place_kernel(
    lens_ref, arrive_ref, slot_ref, entry_ref, cache_ref, landed_ref, out_ref,
    rows_ref, in_sems, out_sems,
):
    rows = out_ref.shape[0]

    def copy_in(row, source, source_row):
        return pltpu.make_async_copy(source.at[source_row], rows_ref.at[row], in_sems.at[row])

    def copy_out(row):
        return pltpu.make_async_copy(rows_ref.at[row], out_ref.at[row], out_sems.at[row])

    def begin(row, carry):
        @pl.when(arrive_ref[row] == 0)
        def _():
            copy_in(row, cache_ref, row).start()

        @pl.when(arrive_ref[row] != 0)
        def _():
            copy_in(row, landed_ref, slot_ref[row]).start()

        return carry

    def renew(row, carry):
        copy_in(row, cache_ref, row).wait()
        start = pl.multiple_of(lens_ref[row] // WINDOW * WINDOW, WINDOW)
        window = rows_ref.at[row, pl.ds(start, WINDOW)]
        position = lax.broadcasted_iota(jnp.int32, window.shape, 0) + start
        window[...] = jnp.where(position == lens_ref[row], entry_ref[row], window[...])
        copy_out(row).start()
        return carry

    def finish(row, carry):
        copy_out(row).wait()
        return carry

    lax.fori_loop(0, rows, begin, 0)
    lax.fori_loop(0, rows, renew, 0)
    lax.fori_loop(0, rows, finish, 0)


def place_cache(lengths, arriving, landed_slot, entries, cache_kv, landed):
    rows, length_cap, entry_width = cache_kv.shape
    return pl.pallas_call(
        place_kernel,
        grid_spec=pltpu.PrefetchScalarGridSpec(
            num_scalar_prefetch=3,
            grid=(1,),
            in_specs=[
                pl.BlockSpec((rows, 1, entry_width), lambda i, a, b, c: (0, 0, 0)),
                pl.BlockSpec(memory_space=pl.ANY),
                pl.BlockSpec(memory_space=pl.ANY),
            ],
            out_specs=pl.BlockSpec(memory_space=pl.ANY),
            scratch_shapes=[
                pltpu.VMEM((rows, length_cap, entry_width), BF16),
                pltpu.SemaphoreType.DMA((rows,)),
                pltpu.SemaphoreType.DMA((rows,)),
            ],
        ),
        out_shape=jax.ShapeDtypeStruct(cache_kv.shape, BF16),
        compiler_params=pltpu.CompilerParams(vmem_limit_bytes=VMEM_BYTES),
        cost_estimate=pl.CostEstimate(
            flops=0, bytes_accessed=cache_kv.size * 4, transcendentals=0
        ),
        name="place_cache",
    )(lengths, arriving.astype(jnp.int32), landed_slot, entries[:, None, :], cache_kv, landed)


def pick_kernel(slot_ref, *refs):
    count = len(refs) // 2
    for source, target in zip(refs[:count], refs[count:]):
        target[...] = source[...]


def pick_caches(slots, cache_kv):
    shifts, count = slots.shape
    block = (1,) + cache_kv.shape[1:]
    return pl.pallas_call(
        pick_kernel,
        grid_spec=pltpu.PrefetchScalarGridSpec(
            num_scalar_prefetch=1,
            grid=(count,),
            in_specs=[
                pl.BlockSpec(block, lambda i, slots, k=k: (slots[k, i], 0, 0))
                for k in range(shifts)
            ],
            out_specs=[pl.BlockSpec(block, lambda i, slots: (i, 0, 0)) for k in range(shifts)],
        ),
        out_shape=[
            jax.ShapeDtypeStruct((count,) + cache_kv.shape[1:], BF16) for k in range(shifts)
        ],
        compiler_params=pltpu.CompilerParams(vmem_limit_bytes=VMEM_BYTES),
        cost_estimate=pl.CostEstimate(
            flops=0,
            bytes_accessed=4 * shifts * count * cache_kv.shape[1] * cache_kv.shape[2],
            transcendentals=0,
        ),
        name="pick_caches",
    )(slots, *([cache_kv] * shifts))


def exchange(array, groups=PLANES):
    return lax.all_to_all(array, "cuts", 0, 0, tiled=True, axis_index_groups=groups)


def behind(array, *marks):
    return lax.optimization_barrier((array, *marks))[0]


def swap_cores(array):
    return lax.ppermute(array, "inst", [(g, g ^ 1) for g in range(4)])


def rows_kernel(places_ref, *refs, counts):
    weights_ref, out_ref = refs[sum(counts)], refs[-1]
    first = 0
    for step, count in enumerate(counts):
        pieces = refs[first : first + count]
        first += count

        @pl.when(pl.program_id(0) == step)
        def _(pieces=pieces):
            at = 0
            for piece in pieces:
                lines, rows, width = piece.shape
                total = jnp.dot(
                    piece[...].reshape(lines * rows, width),
                    weights_ref[...],
                    preferred_element_type=F32,
                )
                out_ref[0, at : at + lines * rows] = total.astype(BF16)
                at += lines * rows


def project_rows(places, groups, weights, into):
    lines, rows, width = groups[0][0].shape
    block = (1, sum(piece.shape[0] for piece in groups[0]) * rows, weights.shape[1])
    pieces = [piece for group in groups for piece in group]
    whole = lambda shape: pl.BlockSpec(shape, lambda i, places: (0,) * len(shape))
    operands = [*pieces, weights]
    in_specs = [whole(operand.shape) for operand in operands]
    if into is not None:
        operands.append(into)
        in_specs.append(pl.BlockSpec(memory_space=pl.ANY))
    return pl.pallas_call(
        functools.partial(rows_kernel, counts=[len(group) for group in groups]),
        grid_spec=pltpu.PrefetchScalarGridSpec(
            num_scalar_prefetch=1,
            grid=(len(groups),),
            in_specs=in_specs,
            out_specs=pl.BlockSpec(block, lambda i, places: (places[i], 0, 0)),
        ),
        out_shape=jax.ShapeDtypeStruct((SIDE,) + block[1:], BF16),
        input_output_aliases={} if into is None else {len(operands): 0},
        compiler_params=pltpu.CompilerParams(vmem_limit_bytes=VMEM_BYTES),
        cost_estimate=pl.CostEstimate(
            flops=2 * len(groups) * block[1] * width * block[2],
            bytes_accessed=2 * (len(groups) * block[1] * width + weights.size),
            transcendentals=0,
        ),
        name="project_rows",
    )(places, *operands)


def out_kernel(heads_ref, *refs):
    out_ref = refs[-1]
    pieces = (len(refs) - 1) // 2
    steps = pl.num_programs(0)

    def add_up(weights):
        total = jnp.dot(heads_ref[0], weights[0][...], preferred_element_type=F32)
        for piece in range(1, pieces):
            total += jnp.dot(heads_ref[piece], weights[piece][...], preferred_element_type=F32)
        out_ref[...] = total.astype(BF16)

    @pl.when(pl.program_id(0) < steps // 2)
    def _():
        add_up(refs[:pieces])

    @pl.when(pl.program_id(0) >= steps // 2)
    def _():
        add_up(refs[pieces : 2 * pieces])


def project_out(heads, mine, other):
    pieces, rows, depth = heads.shape
    half = mine[0].shape[1]
    tile = 512
    steps = half // tile
    first = [pl.BlockSpec((depth, tile), lambda i: (0, jnp.minimum(i, steps - 1)))] * pieces
    second = [pl.BlockSpec((depth, tile), lambda i: (0, jnp.maximum(i - steps, 0)))] * pieces
    return pl.pallas_call(
        out_kernel,
        grid=(2 * steps,),
        in_specs=[pl.BlockSpec((pieces, rows, depth), lambda i: (0, 0, 0))] + first + second,
        out_specs=pl.BlockSpec((rows, tile), lambda i: (0, i)),
        out_shape=jax.ShapeDtypeStruct((rows, 2 * half), BF16),
        compiler_params=pltpu.CompilerParams(vmem_limit_bytes=VMEM_BYTES),
        cost_estimate=pl.CostEstimate(
            flops=4 * rows * pieces * depth * half,
            bytes_accessed=4 * pieces * depth * half,
            transcendentals=0,
        ),
        name="project_out",
    )(heads, *mine, *other)


def body(
    hidden,
    cache_kv,
    cache_len,
    mig_source,
    expert_ids,
    gate_w,
    attn_gain,
    w_query,
    w_keyval,
    q_gain,
    k_gain,
    w_out,
    moe_gain,
    w_gate,
    w_up,
    w_down,
):
    group_count = lax.axis_size("inst")
    cut_count = lax.axis_size("cuts")
    local_rows, width = hidden.shape
    group_total = local_rows * cut_count
    group_id = lax.axis_index("inst")
    cut_id = lax.axis_index("cuts")
    low = cut_id % 2 == 0
    at_x = (cut_id // 2) % SIDE
    at_y = cut_id // (2 * SIDE)
    slot_ids = jnp.arange(local_rows, dtype=jnp.int32)
    own_rows = (group_id * cut_count + cut_id) * local_rows + slot_ids

    facts = jnp.stack([mig_source, cache_len]).astype(F32)
    all_facts = lax.all_to_all(
        jnp.broadcast_to(facts[None], (group_count,) + facts.shape), "inst", 0, 0, tiled=True
    )

    w_keyval_pair = from_pair(w_keyval, 0)
    first_core = group_id % 2 == 0
    half_depth = width // 2
    w_query_part = from_pair(
        lax.dynamic_slice_in_dim(w_query, (group_id % 2) * half_depth, half_depth, 0), 0
    )
    w_query_rest = swap_cores(w_query_part)

    normed = norm_rows(hidden.astype(F32), attn_gain.astype(F32)).astype(BF16)
    half_rows = local_rows // 2
    after, before = shift(normed, 0, SIDE - 1), shift(normed, 0, 1)
    across = jnp.concatenate(
        [shift(after[:half_rows], 0, SIDE - 1), shift(before[half_rows:], 0, 1)]
    )
    line = jnp.zeros((SIDE,) + normed.shape, BF16)
    for offset, rows in enumerate((normed, after, across, before)):
        line = lax.dynamic_update_slice(line, rows[None], ((at_x + offset) % SIDE, 0, 0))
    half_line = SIDE // 2
    after, before = shift(line, SIDE - 1, 0), shift(line, 1, 0)
    across = [shift(after[:half_line], SIDE - 1, 0), shift(before[half_line:], 1, 0)]

    half_width = width // 2
    w_mine = lax.dynamic_slice_in_dim(w_out, (group_id % 2) * half_width, half_width, 1)
    w_here = jnp.concatenate([w_mine, from_pair(w_mine, 1)])
    depth = w_out.shape[0]
    w_after, w_before = shift(w_here, 0, SIDE - 1), shift(w_here, 0, 1)

    w_gate, w_up, w_here = lax.optimization_barrier((w_gate, w_up, w_here))
    one_pair = from_pair(jnp.where(first_core, w_gate, w_up), 1)
    w_down, w_query_rest = lax.optimization_barrier((w_down, w_query_rest))
    w_down_pair = from_pair(w_down, 0)

    w_query_pair = jnp.where(
        first_core,
        jnp.concatenate([w_query_part, w_query_rest]),
        jnp.concatenate([w_query_rest, w_query_part]),
    )
    w_project = lax.optimization_barrier(
        jnp.concatenate([w_query, w_query_pair, w_keyval, w_keyval_pair], axis=1)
    )
    q_width = 2 * w_query.shape[1]
    kv_width = w_keyval.shape[1]

    places = (at_y + jnp.arange(SIDE, dtype=jnp.int32)) % SIDE
    spread = jnp.stack([places[0], places[1], places[3]])
    projected = project_rows(spread, [[line], [after], [before]], w_project, None)
    across = [behind(part, projected) for part in across]
    projected = project_rows(places[2:3], [across], w_project, projected)
    arrived = exchange(projected.reshape(PLANE, local_rows, -1))
    w_after, w_before = behind(w_after, projected), behind(w_before, projected)
    w_across = jnp.concatenate(
        [shift(w_after[:depth], 0, SIDE - 1), shift(w_before[depth:], 0, 1)]
    )
    mine = [w_here, w_after, w_across, w_before]

    goes_to = all_facts[:, 0].astype(jnp.int32) == own_rows[None, :]
    lengths = jnp.sum(jnp.where(goes_to, all_facts[:, 1], 0.0), axis=0).astype(jnp.int32)
    targets = jnp.arange(group_count, dtype=jnp.int32)
    leaving = goes_to & (targets[:, None] != group_id)
    leave_rank = jnp.cumsum(leaving.astype(jnp.int32), axis=1) - 1
    chosen = leaving[:, None, :] & (
        leave_rank[:, None, :] == jnp.arange(MIG, dtype=jnp.int32)[None, :, None]
    )
    send_slot = jnp.sum(jnp.where(chosen, slot_ids[None, None, :], 0), axis=2)
    source_group = mig_source // group_total
    arriving = source_group != group_id
    from_group = (source_group[None, :] == targets[:, None]) & arriving[None, :]
    arrival_rank = jnp.sum(
        jnp.where(from_group, jnp.cumsum(from_group.astype(jnp.int32), axis=1) - 1, 0), axis=0
    )
    source_pick = jnp.where(arriving, source_group, 0)

    shifts = jnp.arange(1, group_count, dtype=jnp.int32)
    picked = pick_caches(send_slot[(group_id + shifts) % group_count], cache_kv)
    landed = jnp.concatenate(
        [
            lax.ppermute(
                array, "inst", [(g, (g + shift) % group_count) for g in range(group_count)]
            )
            for shift, array in zip(range(1, group_count), picked)
        ]
    )
    distance = (group_id - source_group) % group_count
    landed_slot = jnp.where(arriving, (distance - 1) * MIG + arrival_rank, 0)

    other_pair = swap_cores(behind(one_pair, arrived))
    other = [swap_cores(part) for part in mine]

    own_kv = arrived[:, :, q_width : q_width + kv_width]
    pair_kv = arrived[:, :, q_width + kv_width :]
    kv_rows = jnp.where(
        low,
        jnp.concatenate([own_kv, pair_kv], axis=2),
        jnp.concatenate([pair_kv, own_kv], axis=2),
    )
    kv_rows = jnp.transpose(kv_rows, (1, 0, 2)).reshape(local_rows, -1)
    attention, entries = attend(arrived, q_width, kv_rows, cache_kv, 0, lengths, q_gain, k_gain)

    attention = attention.reshape(SIDE, SIDE, local_rows, q_width)
    attention = lax.dynamic_slice_in_dim(
        jnp.concatenate([attention, attention], axis=1), at_x, SIDE, 1
    )
    heads = exchange(attention, COLUMNS)
    heads = behind(heads, one_pair, w_down_pair, *picked)
    heads = jnp.transpose(heads, (1, 0, 2, 3)).reshape(SIDE, SIDE * local_rows, q_width)
    partial_value = project_out(heads, mine, other)
    sums = exchange(partial_value.reshape(SIDE, local_rows, width), COLUMNS)

    got_entries = lax.all_to_all(entries[send_slot], "inst", 0, 0, tiled=True)
    new_entries = jnp.where(arriving[:, None], got_entries[source_pick, arrival_rank], entries)
    sums = behind(sums, new_entries, landed, other_pair)

    attn_out = jnp.sum(sums.astype(F32), axis=0)
    mine_out, other_out = attn_out[:, :half_width], attn_out[:, half_width:]
    mixed_rows = hidden.astype(F32) + jnp.concatenate(
        [jnp.where(first_core, mine_out, other_out), jnp.where(first_core, other_out, mine_out)],
        axis=1,
    )
    got_rows = lax.all_to_all(mixed_rows[send_slot], "inst", 0, 0, tiled=True)
    mixed_rows = jnp.where(arriving[:, None], got_rows[source_pick, arrival_rank], mixed_rows)
    moe_local = norm_rows(mixed_rows, moe_gain.astype(F32)).astype(BF16)

    expert_range = jnp.arange(PLANE, dtype=jnp.int32)
    combine = jnp.sum(
        jnp.where(
            expert_ids[:, :, None] == expert_range[None, None, :],
            gate_w.astype(F32)[:, :, None],
            0.0,
        ),
        axis=1,
    )
    flags = jnp.transpose(combine) > 0.0
    rank = jnp.cumsum(flags.astype(jnp.int32), axis=1) - 1
    slot_range = jnp.arange(MOST, dtype=jnp.int32)
    match = flags[:, None, :] & (rank[:, None, :] == slot_range[None, :, None])
    match = match.reshape(PLANE * MOST, local_rows)
    slab = jnp.dot(match.astype(BF16), moe_local, preferred_element_type=F32).astype(BF16)
    slab_rows = exchange(slab.reshape(PLANE, MOST, width)).reshape(PLANE * MOST, width)
    cache_next = place_cache(cache_len, arriving, landed_slot, new_entries, cache_kv, landed)
    slab_rows = behind(slab_rows, cache_next)

    def expert_half(gate_part, upward, down):
        activation = (jax.nn.silu(gate_part) * upward).astype(BF16)
        return jnp.dot(activation, down, preferred_element_type=F32)

    own_gate = jnp.dot(slab_rows, w_gate, preferred_element_type=F32)
    own_up = jnp.dot(slab_rows, w_up, preferred_element_type=F32)
    pair_one = jnp.dot(slab_rows, one_pair, preferred_element_type=F32)
    pair_other = jnp.dot(slab_rows, other_pair, preferred_element_type=F32)
    pair_gate = jnp.where(first_core, pair_one, pair_other)
    pair_up = jnp.where(first_core, pair_other, pair_one)
    expert_out = (
        expert_half(own_gate, own_up, w_down) + expert_half(pair_gate, pair_up, w_down_pair)
    ).astype(BF16)
    returned = exchange(expert_out.reshape(PLANE, MOST, width)).reshape(PLANE * MOST, width)
    slot_gate = jnp.where(
        match, jnp.repeat(jnp.transpose(combine), MOST, axis=0), 0.0
    ).astype(BF16)
    moe_out = lax.dot_general(
        slot_gate, returned, (((0,), (0,)), ((), ())), preferred_element_type=F32
    )
    hidden_next = (mixed_rows + moe_out).astype(BF16)
    return (hidden_next, cache_next)


def solution(mesh):
    in_specs = (
        P(("inst", "cuts"), None),
        P(("inst", "cuts"), None, None),
        P(("inst", "cuts")),
        P(("inst", "cuts")),
        P(("inst", "cuts"), None),
        P(("inst", "cuts"), None),
        P(),
        P(None, "cuts"),
        P(None, "cuts"),
        P(),
        P(),
        P("cuts", None),
        P(),
        P(None, "cuts"),
        P(None, "cuts"),
        P("cuts", None),
    )
    out_specs = (P(("inst", "cuts"), None), P(("inst", "cuts"), None, None))
    return jax.shard_map(body, mesh=mesh, in_specs=in_specs, out_specs=out_specs, check_vma=False)
```

```python
import functools
import jax
import jax.numpy as jnp
from jax import lax
from jax.experimental import pallas as pl
from jax.experimental.pallas import tpu as pltpu
from jax.sharding import PartitionSpec as P

HD = 128
MIG = 2
MOST = 4
EPSILON = 1e-06
ROPE_BASE = 1000000.0
SIDE = 4
PLANE = SIDE * SIDE
VMEM_BYTES = 56 * 1024 * 1024
BF16 = jnp.bfloat16
F32 = jnp.float32


def cut_index(y, x, z):
    return (y * SIDE + x) * 2 + z


PLANES = [[cut_index(y, x, z) for y in range(SIDE) for x in range(SIDE)] for z in range(2)]
BLOCKS = [
    [cut_index(y, x, z) for y in range(SIDE) for x in (first, first + 1)]
    for first in (0, 2)
    for z in range(2)
]


def shift(array, dy, dx):
    moves = [
        (cut_index(y, x, z), cut_index((y + dy) % SIDE, (x + dx) % SIDE, z))
        for y in range(SIDE)
        for x in range(SIDE)
        for z in range(2)
    ]
    return lax.ppermute(array, "cuts", moves)


def mirror(array):
    moves = [
        (cut_index(y, x, z), cut_index(y, SIDE - 1 - x, z))
        for y in range(SIDE)
        for x in range(SIDE)
        for z in range(2)
    ]
    return lax.ppermute(array, "cuts", moves)


def pair_perm(side):
    out = []
    for z in range(4):
        for core in range(2):
            way = (side + core) % 2
            other = z ^ 1 if way == 0 else (z + 1 if z % 2 else z - 1) % 4
            for y in range(SIDE):
                for x in range(SIDE):
                    out.append(
                        (
                            ((z // 2) * 2 + core) * 32 + cut_index(y, x, z % 2),
                            ((other // 2) * 2 + core) * 32 + cut_index(y, x, other % 2),
                        )
                    )
    return out


def from_pair(array, side):
    return lax.ppermute(array, ("inst", "cuts"), pair_perm(side))


def norm_rows(values, gain_vec):
    mean_square = jnp.mean(values * values, axis=-1, keepdims=True)
    return values * lax.rsqrt(mean_square + EPSILON) * gain_vec


def attend_kernel(
    lens_ref, q_ref, kv_ref, gcos_ref, gsin_ref, kcos_ref, ksin_ref, turn_ref, cache_ref,
    att_ref, entry_ref, qs_ref, es_ref, os_ref, *, rows_step, kv_count, group_size,
):
    step = pl.program_id(0)
    peers, rows = q_ref.shape[:2]
    per_peer = att_ref.shape[2] // HD
    length_cap = cache_ref.shape[1]
    width = kv_count * HD
    ones = jnp.ones((HD, HD), BF16)

    @pl.when(step == 0)
    def _():
        def prepare(heads, cosine, sine):
            stacked = jnp.concatenate(heads, axis=0)
            values = stacked.astype(F32)
            squares = values * values
            high = squares.astype(BF16)
            low = (squares - high.astype(F32)).astype(BF16)
            total = jnp.dot(high, ones, preferred_element_type=F32)
            total += jnp.dot(low, ones, preferred_element_type=F32)
            turned = jnp.dot(stacked, turn_ref[...], preferred_element_type=F32)
            inverse = lax.rsqrt(total * (1.0 / HD) + EPSILON)
            count = len(heads)
            cosine = jnp.concatenate([cosine] * count, axis=0)
            sine = jnp.concatenate([sine] * count, axis=0)
            return (values * cosine + turned * sine) * inverse

        gcos, gsin = gcos_ref[...], gsin_ref[...]
        for p in range(peers):
            heads = [q_ref[p, :, j * HD : (j + 1) * HD] for j in range(per_peer)]
            ready = prepare(heads, gcos, gsin)
            for j in range(per_peer):
                qs_ref[:, p * per_peer + j, :] = ready[j * rows : (j + 1) * rows]
        heads = [kv_ref[:, k * HD : (k + 1) * HD] for k in range(kv_count)]
        keys = prepare(heads, kcos_ref[...], ksin_ref[...]).astype(BF16)
        for k in range(kv_count):
            key = keys[k * rows : (k + 1) * rows]
            entry_ref[:, k * HD : (k + 1) * HD] = key
            es_ref[:, k, :] = key.astype(F32)
            value = kv_ref[:, width + k * HD : width + (k + 1) * HD]
            entry_ref[:, width + k * HD : width + (k + 1) * HD] = value
            es_ref[:, kv_count + k, :] = value.astype(F32)

    scale = HD ** (-0.5)
    heads = kv_count * group_size
    positions = lax.broadcasted_iota(jnp.int32, (heads, length_cap), 1)
    places = lax.broadcasted_iota(jnp.int32, (length_cap, 2 * width), 0)
    spans = [slice(k * group_size, (k + 1) * group_size) for k in range(kv_count)]
    first = step * rows_step
    blocks, scores, weights, results = [], [], [], []
    for i in range(rows_step):
        entry = es_ref[first + i]
        entry = jnp.concatenate(
            [entry[k : k + 1] for k in range(2 * kv_count)], axis=1
        ).astype(BF16)
        blocks.append(jnp.where(places == lens_ref[first + i], entry, cache_ref[i]))
    for i in range(rows_step):
        queries = qs_ref[first + i].astype(BF16)
        scores.append(
            jnp.concatenate(
                [
                    lax.dot_general(
                        queries[spans[k]], blocks[i][:, k * HD : (k + 1) * HD],
                        (((1,), (1,)), ((), ())), preferred_element_type=F32,
                    )
                    for k in range(kv_count)
                ],
                axis=0,
            )
        )
    for i in range(rows_step):
        score = jnp.where(positions <= lens_ref[first + i], scores[i] * scale, -1e30)
        peak = jnp.max(score, axis=1, keepdims=True)
        weights.append(jnp.exp(score - peak).astype(BF16))
    for i in range(rows_step):
        total = jnp.dot(weights[i], ones, preferred_element_type=F32)
        summed = jnp.concatenate(
            [
                jnp.dot(
                    weights[i][spans[k]],
                    blocks[i][:, width + k * HD : width + (k + 1) * HD],
                    preferred_element_type=F32,
                )
                for k in range(kv_count)
            ],
            axis=0,
        )
        results.append(summed / total)
    for i in range(rows_step):
        os_ref[first + i] = results[i]

    @pl.when(step == pl.num_programs(0) - 1)
    def _():
        for p in range(peers):
            for j in range(per_peer):
                att_ref[p, :, j * HD : (j + 1) * HD] = os_ref[:, p * per_peer + j, :].astype(BF16)


def attend(q_peers, q_width, kv_rows, cache_kv, lengths, q_gain, k_gain):
    peers, rows, sent_width = q_peers.shape
    length_cap, entry_width = cache_kv.shape[1:]
    kv_count = entry_width // (2 * HD)
    heads = peers * q_width // HD
    rows_step = 8
    half = HD // 2
    frequency = ROPE_BASE ** (-2.0 * jnp.arange(half, dtype=F32) / HD)
    angles = lengths.astype(F32)[:, None] * frequency[None, :]
    cosine = jnp.concatenate([jnp.cos(angles), jnp.cos(angles)], axis=-1)
    sine = jnp.concatenate([jnp.sin(angles), jnp.sin(angles)], axis=-1)
    turn = (jnp.eye(HD, k=half) - jnp.eye(HD, k=-half)).astype(BF16)
    tables = [
        table * gain[None, :]
        for gain in (q_gain, k_gain)
        for table, gain in ((cosine, gain), (sine, jnp.roll(gain, half)))
    ]
    whole = lambda shape: pl.BlockSpec(shape, lambda i, lens: (0,) * len(shape))
    return pl.pallas_call(
        functools.partial(
            attend_kernel, rows_step=rows_step, kv_count=kv_count, group_size=heads // kv_count
        ),
        grid_spec=pltpu.PrefetchScalarGridSpec(
            num_scalar_prefetch=1,
            grid=(rows // rows_step,),
            in_specs=[
                whole((peers, rows, sent_width)),
                whole((rows, entry_width)),
                whole((rows, HD)),
                whole((rows, HD)),
                whole((rows, HD)),
                whole((rows, HD)),
                whole((HD, HD)),
                pl.BlockSpec((rows_step, length_cap, entry_width), lambda i, lens: (i, 0, 0)),
            ],
            out_specs=[whole((peers, rows, q_width)), whole((rows, entry_width))],
            scratch_shapes=[
                pltpu.VMEM((rows, heads, HD), F32),
                pltpu.VMEM((rows, 2 * kv_count, HD), F32),
                pltpu.VMEM((rows, heads, HD), F32),
            ],
        ),
        out_shape=[
            jax.ShapeDtypeStruct((peers, rows, q_width), BF16),
            jax.ShapeDtypeStruct((rows, entry_width), BF16),
        ],
        compiler_params=pltpu.CompilerParams(vmem_limit_bytes=VMEM_BYTES),
        cost_estimate=pl.CostEstimate(
            flops=4 * rows * heads * HD * length_cap,
            bytes_accessed=cache_kv.size * 2 + q_peers.size * 4,
            transcendentals=rows * heads * length_cap,
        ),
        name="attend",
    )(lengths, q_peers, kv_rows, *tables, turn, cache_kv)


WINDOW = 16


def place_kernel(
    lens_ref, distance_ref, rank_ref, entry_ref, cache_ref, *refs,
):
    *landed_refs, out_ref, rows_ref, in_sems, out_sems = refs
    rows = out_ref.shape[0]

    def copy_in(row, source, source_row):
        return pltpu.make_async_copy(source.at[source_row], rows_ref.at[row], in_sems.at[row])

    def copy_out(row):
        return pltpu.make_async_copy(rows_ref.at[row], out_ref.at[row], out_sems.at[row])

    def begin(row, carry):
        @pl.when(distance_ref[row] == 0)
        def _():
            copy_in(row, cache_ref, row).start()

        for distance, landed_ref in enumerate(landed_refs, 1):

            @pl.when(distance_ref[row] == distance)
            def _(landed_ref=landed_ref):
                copy_in(row, landed_ref, rank_ref[row]).start()

        return carry

    def renew(row, carry):
        copy_in(row, cache_ref, row).wait()
        start = pl.multiple_of(lens_ref[row] // WINDOW * WINDOW, WINDOW)
        window = rows_ref.at[row, pl.ds(start, WINDOW)]
        position = lax.broadcasted_iota(jnp.int32, window.shape, 0) + start
        window[...] = jnp.where(position == lens_ref[row], entry_ref[row], window[...])
        copy_out(row).start()
        return carry

    def finish(row, carry):
        copy_out(row).wait()
        return carry

    lax.fori_loop(0, rows, begin, 0)
    lax.fori_loop(0, rows, renew, 0)
    lax.fori_loop(0, rows, finish, 0)


def place_cache(lengths, distance, rank, entries, cache_kv, landed):
    rows, length_cap, entry_width = cache_kv.shape
    return pl.pallas_call(
        place_kernel,
        grid_spec=pltpu.PrefetchScalarGridSpec(
            num_scalar_prefetch=3,
            grid=(1,),
            in_specs=[
                pl.BlockSpec((rows, 1, entry_width), lambda i, a, b, c: (0, 0, 0)),
            ]
            + [pl.BlockSpec(memory_space=pl.ANY)] * (1 + len(landed)),
            out_specs=pl.BlockSpec(memory_space=pl.ANY),
            scratch_shapes=[
                pltpu.VMEM((rows, length_cap, entry_width), BF16),
                pltpu.SemaphoreType.DMA((rows,)),
                pltpu.SemaphoreType.DMA((rows,)),
            ],
        ),
        out_shape=jax.ShapeDtypeStruct(cache_kv.shape, BF16),
        compiler_params=pltpu.CompilerParams(vmem_limit_bytes=VMEM_BYTES),
        cost_estimate=pl.CostEstimate(
            flops=0, bytes_accessed=cache_kv.size * 4, transcendentals=0
        ),
        name="place_cache",
    )(lengths, distance, rank, entries[:, None, :], cache_kv, *landed)


def pick_kernel(slot_ref, *refs):
    count = len(refs) // 2
    for source, target in zip(refs[:count], refs[count:]):
        target[...] = source[...]


def pick_caches(slots, cache_kv):
    shifts, count = slots.shape
    block = (1,) + cache_kv.shape[1:]
    return pl.pallas_call(
        pick_kernel,
        grid_spec=pltpu.PrefetchScalarGridSpec(
            num_scalar_prefetch=1,
            grid=(count,),
            in_specs=[
                pl.BlockSpec(block, lambda i, slots, k=k: (slots[k, i], 0, 0))
                for k in range(shifts)
            ],
            out_specs=[pl.BlockSpec(block, lambda i, slots: (i, 0, 0)) for k in range(shifts)],
        ),
        out_shape=[
            jax.ShapeDtypeStruct((count,) + cache_kv.shape[1:], BF16) for k in range(shifts)
        ],
        compiler_params=pltpu.CompilerParams(vmem_limit_bytes=VMEM_BYTES),
        cost_estimate=pl.CostEstimate(
            flops=0,
            bytes_accessed=4 * shifts * count * cache_kv.shape[1] * cache_kv.shape[2],
            transcendentals=0,
        ),
        name="pick_caches",
    )(slots, *([cache_kv] * shifts))


def exchange(array, groups=PLANES):
    return lax.all_to_all(array, "cuts", 0, 0, tiled=True, axis_index_groups=groups)


def behind(array, *marks):
    return lax.optimization_barrier((array, *marks))[0]


def swap_cores(array):
    return lax.ppermute(array, "inst", [(g, g ^ 1) for g in range(4)])


def rows_kernel(places_ref, *refs):
    *pieces, weights_ref, out_ref, rows_ref, total_ref = refs
    step = pl.program_id(0)
    at = 0
    for piece in pieces:
        count = piece.shape[0] * piece.shape[1]
        rows_ref[at : at + count] = piece[...].reshape(count, piece.shape[2])
        at += count
    part = jnp.dot(rows_ref[...], weights_ref[...], preferred_element_type=F32)

    @pl.when(step == 0)
    def _():
        total_ref[...] = part

    @pl.when(step > 0)
    def _():
        total_ref[...] += part

    @pl.when(step == pl.num_programs(0) - 1)
    def _():
        lines = out_ref.shape[1]
        for line in range(out_ref.shape[0]):
            out_ref[places_ref[line]] = total_ref[line * lines : (line + 1) * lines].astype(BF16)


def project_rows(places, pieces, weights):
    rows = sum(piece.shape[0] * piece.shape[1] for piece in pieces)
    width, columns = weights.shape
    depth = width // 4
    out = (SIDE, rows // SIDE, columns)
    return pl.pallas_call(
        rows_kernel,
        grid_spec=pltpu.PrefetchScalarGridSpec(
            num_scalar_prefetch=1,
            grid=(width // depth,),
            in_specs=[
                pl.BlockSpec(piece.shape[:2] + (depth,), lambda i, places: (0, 0, i))
                for piece in pieces
            ]
            + [pl.BlockSpec((depth, columns), lambda i, places: (i, 0))],
            out_specs=pl.BlockSpec(out, lambda i, places: (0, 0, 0)),
            scratch_shapes=[pltpu.VMEM((rows, depth), BF16), pltpu.VMEM((rows, columns), F32)],
        ),
        out_shape=jax.ShapeDtypeStruct(out, BF16),
        compiler_params=pltpu.CompilerParams(vmem_limit_bytes=VMEM_BYTES),
        cost_estimate=pl.CostEstimate(
            flops=2 * rows * width * columns,
            bytes_accessed=2 * (rows * width + weights.size),
            transcendentals=0,
        ),
        name="project_rows",
    )(places, *pieces, weights)


def out_kernel(heads_ref, *refs, spots):
    out_ref = refs[-1]
    sources, _, rows, _ = heads_ref.shape
    steps = pl.num_programs(0)

    def add_up(weights):
        total = 0.0
        for (offset, first), piece in zip(spots, weights):
            depth = piece.shape[0]
            heads = heads_ref[:, offset].reshape(sources * rows, -1)[:, first : first + depth]
            total += jnp.dot(heads, piece[...], preferred_element_type=F32)
        out_ref[...] = total.astype(BF16)

    @pl.when(pl.program_id(0) < steps // 2)
    def _():
        add_up(refs[: len(spots)])

    @pl.when(pl.program_id(0) >= steps // 2)
    def _():
        add_up(refs[len(spots) : 2 * len(spots)])


def project_out(heads, spots, mine, other):
    sources, _, rows, _ = heads.shape
    half = mine[0].shape[1]
    tile = 512
    steps = half // tile
    first = [
        pl.BlockSpec((part.shape[0], tile), lambda i: (0, jnp.minimum(i, steps - 1)))
        for part in mine
    ]
    second = [
        pl.BlockSpec((part.shape[0], tile), lambda i: (0, jnp.maximum(i - steps, 0)))
        for part in other
    ]
    return pl.pallas_call(
        functools.partial(out_kernel, spots=spots),
        grid=(2 * steps,),
        in_specs=[pl.BlockSpec(heads.shape, lambda i: (0, 0, 0, 0))] + first + second,
        out_specs=pl.BlockSpec((sources * rows, tile), lambda i: (0, i)),
        out_shape=jax.ShapeDtypeStruct((sources * rows, 2 * half), BF16),
        compiler_params=pltpu.CompilerParams(vmem_limit_bytes=VMEM_BYTES),
        cost_estimate=pl.CostEstimate(
            flops=2 * heads.size * 2 * half,
            bytes_accessed=4 * sum(part.size for part in mine),
            transcendentals=0,
        ),
        name="project_out",
    )(heads, *mine, *other)


def body(
    hidden,
    cache_kv,
    cache_len,
    mig_source,
    expert_ids,
    gate_w,
    attn_gain,
    w_query,
    w_keyval,
    q_gain,
    k_gain,
    w_out,
    moe_gain,
    w_gate,
    w_up,
    w_down,
):
    group_count = lax.axis_size("inst")
    cut_count = lax.axis_size("cuts")
    local_rows, width = hidden.shape
    group_total = local_rows * cut_count
    group_id = lax.axis_index("inst")
    cut_id = lax.axis_index("cuts")
    low = cut_id % 2 == 0
    at_x = (cut_id // 2) % SIDE
    at_y = cut_id // (2 * SIDE)
    slot_ids = jnp.arange(local_rows, dtype=jnp.int32)
    own_rows = (group_id * cut_count + cut_id) * local_rows + slot_ids

    facts = jnp.stack([mig_source, cache_len]).astype(F32)
    all_facts = lax.all_to_all(
        jnp.broadcast_to(facts[None], (group_count,) + facts.shape), "inst", 0, 0, tiled=True
    )

    w_keyval_pair = from_pair(w_keyval, 0)
    first_core = group_id % 2 == 0
    half_depth = width // 2
    w_query_part = from_pair(
        lax.dynamic_slice_in_dim(w_query, (group_id % 2) * half_depth, half_depth, 0), 0
    )
    w_query_rest = swap_cores(w_query_part)

    normed = norm_rows(hidden.astype(F32), attn_gain.astype(F32)).astype(BF16)
    half_rows = local_rows // 2
    after, before = shift(normed, 0, SIDE - 1), shift(normed, 0, 1)
    across = jnp.concatenate(
        [shift(after[:half_rows], 0, SIDE - 1), shift(before[half_rows:], 0, 1)]
    )
    line = jnp.zeros((SIDE,) + normed.shape, BF16)
    for offset, rows in enumerate((normed, after, across, before)):
        line = lax.dynamic_update_slice(line, rows[None], ((at_x + offset) % SIDE, 0, 0))
    half_line = SIDE // 2
    after, before = shift(line, SIDE - 1, 0), shift(line, 1, 0)
    across = [shift(after[:half_line], SIDE - 1, 0), shift(before[half_line:], 1, 0)]

    half_width = width // 2
    w_mine = lax.dynamic_slice_in_dim(w_out, (group_id % 2) * half_width, half_width, 1)
    w_here = jnp.concatenate([w_mine, from_pair(w_mine, 1)])
    w_there = mirror(w_here)

    w_gate, w_up, w_here = lax.optimization_barrier((w_gate, w_up, w_here))
    one_pair = from_pair(jnp.where(first_core, w_gate, w_up), 1)
    w_down, w_query_rest = lax.optimization_barrier((w_down, w_query_rest))
    w_down_pair = from_pair(w_down, 0)

    w_query_pair = jnp.where(
        first_core,
        jnp.concatenate([w_query_part, w_query_rest]),
        jnp.concatenate([w_query_rest, w_query_part]),
    )
    w_project = lax.optimization_barrier(
        jnp.concatenate([w_query, w_query_pair, w_keyval, w_keyval_pair], axis=1)
    )
    q_width = 2 * w_query.shape[1]
    kv_width = w_keyval.shape[1]

    places = (at_y + jnp.arange(SIDE, dtype=jnp.int32)) % SIDE
    projected = project_rows(places, [line, after, *across, before], w_project)
    arrived = exchange(projected.reshape(PLANE, local_rows, -1))

    goes_to = all_facts[:, 0].astype(jnp.int32) == own_rows[None, :]
    lengths = jnp.sum(jnp.where(goes_to, all_facts[:, 1], 0.0), axis=0).astype(jnp.int32)
    targets = jnp.arange(group_count, dtype=jnp.int32)
    leaving = goes_to & (targets[:, None] != group_id)
    leave_rank = jnp.cumsum(leaving.astype(jnp.int32), axis=1) - 1
    chosen = leaving[:, None, :] & (
        leave_rank[:, None, :] == jnp.arange(MIG, dtype=jnp.int32)[None, :, None]
    )
    send_slot = jnp.sum(jnp.where(chosen, slot_ids[None, None, :], 0), axis=2)
    source_group = mig_source // group_total
    arriving = source_group != group_id
    from_group = (source_group[None, :] == targets[:, None]) & arriving[None, :]
    arrival_rank = jnp.sum(
        jnp.where(from_group, jnp.cumsum(from_group.astype(jnp.int32), axis=1) - 1, 0), axis=0
    )
    source_pick = jnp.where(arriving, source_group, 0)


    own_kv = arrived[:, :, q_width : q_width + kv_width]
    pair_kv = arrived[:, :, q_width + kv_width :]
    kv_rows = jnp.where(
        low,
        jnp.concatenate([own_kv, pair_kv], axis=2),
        jnp.concatenate([pair_kv, own_kv], axis=2),
    )
    kv_rows = jnp.transpose(kv_rows, (1, 0, 2)).reshape(local_rows, -1)
    attention, entries = attend(arrived, q_width, kv_rows, cache_kv, lengths, q_gain, k_gain)

    attention = attention.reshape(SIDE, 2, 2, local_rows, q_width)
    left = at_x < 2
    near = jnp.where(left, attention[:, 0], attention[:, 1])
    far = jnp.where(left, attention[:, 1], attention[:, 0])[:, ::-1]
    attention = jnp.stack([near, far], axis=2).reshape(2 * SIDE, 2, local_rows, q_width)
    heads = exchange(attention, BLOCKS)
    heads = behind(heads, w_down_pair)
    other_pair = swap_cores(behind(one_pair, heads))
    mine = [w_here, w_there]
    other = [swap_cores(behind(part, projected)) for part in mine]
    partial_value = project_out(heads, [(0, 0), (1, 0)], mine, other)
    sums = exchange(partial_value.reshape(2 * SIDE, local_rows, width), BLOCKS)

    sums = behind(sums, other_pair)

    attn_out = jnp.sum(sums.astype(F32), axis=0)
    mine_out, other_out = attn_out[:, :half_width], attn_out[:, half_width:]
    mixed_rows = hidden.astype(F32) + jnp.concatenate(
        [jnp.where(first_core, mine_out, other_out), jnp.where(first_core, other_out, mine_out)],
        axis=1,
    )
    rows_entries = jnp.concatenate([mixed_rows, entries.astype(F32)], axis=1)
    got_rows = lax.all_to_all(rows_entries[send_slot], "inst", 0, 0, tiled=True)
    rows_entries = jnp.where(
        arriving[:, None], got_rows[source_pick, arrival_rank], rows_entries
    )
    mixed_rows = rows_entries[:, :width]
    new_entries = rows_entries[:, width:].astype(BF16)

    shifts = jnp.arange(1, group_count, dtype=jnp.int32)
    picked = pick_caches(
        behind(send_slot, got_rows)[(group_id + shifts) % group_count], cache_kv
    )
    landed = [
        lax.ppermute(
            array, "inst", [(g, (g + distance) % group_count) for g in range(group_count)]
        )
        for distance, array in zip(range(1, group_count), picked)
    ]
    distance = (group_id - source_group) % group_count
    cache_next = place_cache(cache_len, distance, arrival_rank, new_entries, cache_kv, landed)

    moe_local = norm_rows(mixed_rows, moe_gain.astype(F32)).astype(BF16)

    expert_range = jnp.arange(PLANE, dtype=jnp.int32)
    combine = jnp.sum(
        jnp.where(
            expert_ids[:, :, None] == expert_range[None, None, :],
            gate_w.astype(F32)[:, :, None],
            0.0,
        ),
        axis=1,
    )
    flags = jnp.transpose(combine) > 0.0
    rank = jnp.cumsum(flags.astype(jnp.int32), axis=1) - 1
    slot_range = jnp.arange(MOST, dtype=jnp.int32)
    match = flags[:, None, :] & (rank[:, None, :] == slot_range[None, :, None])
    match = match.reshape(PLANE * MOST, local_rows)
    slab = jnp.dot(match.astype(BF16), moe_local, preferred_element_type=F32).astype(BF16)
    slab_rows = exchange(slab.reshape(PLANE, MOST, width)).reshape(PLANE * MOST, width)
    slab_rows = behind(slab_rows, *picked)

    def expert_half(gate_part, upward, down):
        activation = (jax.nn.silu(gate_part) * upward).astype(BF16)
        return jnp.dot(activation, down, preferred_element_type=F32)

    own_gate = jnp.dot(slab_rows, w_gate, preferred_element_type=F32)
    own_up = jnp.dot(slab_rows, w_up, preferred_element_type=F32)
    pair_one = jnp.dot(slab_rows, one_pair, preferred_element_type=F32)
    pair_other = jnp.dot(slab_rows, other_pair, preferred_element_type=F32)
    pair_gate = jnp.where(first_core, pair_one, pair_other)
    pair_up = jnp.where(first_core, pair_other, pair_one)
    expert_out = (
        expert_half(own_gate, own_up, w_down) + expert_half(pair_gate, pair_up, w_down_pair)
    ).astype(BF16)
    returned = exchange(expert_out.reshape(PLANE, MOST, width)).reshape(PLANE * MOST, width)
    returned = behind(returned, cache_next)
    slot_gate = jnp.where(
        match, jnp.repeat(jnp.transpose(combine), MOST, axis=0), 0.0
    ).astype(BF16)
    moe_out = lax.dot_general(
        slot_gate, returned, (((0,), (0,)), ((), ())), preferred_element_type=F32
    )
    hidden_next = (mixed_rows + moe_out).astype(BF16)
    return (hidden_next, cache_next)


def solution(mesh):
    in_specs = (
        P(("inst", "cuts"), None),
        P(("inst", "cuts"), None, None),
        P(("inst", "cuts")),
        P(("inst", "cuts")),
        P(("inst", "cuts"), None),
        P(("inst", "cuts"), None),
        P(),
        P(None, "cuts"),
        P(None, "cuts"),
        P(),
        P(),
        P("cuts", None),
        P(),
        P(None, "cuts"),
        P(None, "cuts"),
        P("cuts", None),
    )
    out_specs = (P(("inst", "cuts"), None), P(("inst", "cuts"), None, None))
    return jax.shard_map(body, mesh=mesh, in_specs=in_specs, out_specs=out_specs, check_vma=False)
```

```python
import functools
import jax
import jax.numpy as jnp
from jax import lax
from jax.experimental import pallas as pl
from jax.experimental.pallas import tpu as pltpu
from jax.sharding import PartitionSpec as P

HD = 128
MIG = 2
MOST = 4
EPSILON = 1e-06
ROPE_BASE = 1000000.0
SIDE = 4
PLANE = SIDE * SIDE
VMEM_BYTES = 56 * 1024 * 1024
BF16 = jnp.bfloat16
F32 = jnp.float32


def cut_index(y, x, z):
    return (y * SIDE + x) * 2 + z


PLANES = [[cut_index(y, x, z) for y in range(SIDE) for x in range(SIDE)] for z in range(2)]
BLOCKS = [
    [cut_index(y, x, z) for y in range(SIDE) for x in (first, first + 1)]
    for first in (0, 2)
    for z in range(2)
]


def shift(array, dy, dx):
    moves = [
        (cut_index(y, x, z), cut_index((y + dy) % SIDE, (x + dx) % SIDE, z))
        for y in range(SIDE)
        for x in range(SIDE)
        for z in range(2)
    ]
    return lax.ppermute(array, "cuts", moves)


def mirror(array):
    moves = [
        (cut_index(y, x, z), cut_index(y, SIDE - 1 - x, z))
        for y in range(SIDE)
        for x in range(SIDE)
        for z in range(2)
    ]
    return lax.ppermute(array, "cuts", moves)


def pair_perm(side):
    out = []
    for z in range(4):
        for core in range(2):
            way = (side + core) % 2
            other = z ^ 1 if way == 0 else (z + 1 if z % 2 else z - 1) % 4
            for y in range(SIDE):
                for x in range(SIDE):
                    out.append(
                        (
                            ((z // 2) * 2 + core) * 32 + cut_index(y, x, z % 2),
                            ((other // 2) * 2 + core) * 32 + cut_index(y, x, other % 2),
                        )
                    )
    return out


def from_pair(array, side):
    return lax.ppermute(array, ("inst", "cuts"), pair_perm(side))


def norm_rows(values, gain_vec):
    mean_square = jnp.mean(values * values, axis=-1, keepdims=True)
    return values * lax.rsqrt(mean_square + EPSILON) * gain_vec


def attend_kernel(
    lens_ref, q_ref, kv_ref, gcos_ref, gsin_ref, kcos_ref, ksin_ref, turn_ref, cache_ref,
    att_ref, entry_ref, qs_ref, es_ref, os_ref, *, rows_step, kv_count, group_size,
):
    step = pl.program_id(0)
    peers, rows = q_ref.shape[:2]
    per_peer = att_ref.shape[2] // HD
    length_cap = cache_ref.shape[1]
    width = kv_count * HD
    ones = jnp.ones((HD, HD), BF16)

    @pl.when(step == 0)
    def _():
        def prepare(heads, cosine, sine):
            stacked = jnp.concatenate(heads, axis=0)
            values = stacked.astype(F32)
            squares = values * values
            high = squares.astype(BF16)
            low = (squares - high.astype(F32)).astype(BF16)
            total = jnp.dot(high, ones, preferred_element_type=F32)
            total += jnp.dot(low, ones, preferred_element_type=F32)
            turned = jnp.dot(stacked, turn_ref[...], preferred_element_type=F32)
            inverse = lax.rsqrt(total * (1.0 / HD) + EPSILON)
            count = len(heads)
            cosine = jnp.concatenate([cosine] * count, axis=0)
            sine = jnp.concatenate([sine] * count, axis=0)
            return (values * cosine + turned * sine) * inverse

        gcos, gsin = gcos_ref[...], gsin_ref[...]
        for p in range(peers):
            heads = [q_ref[p, :, j * HD : (j + 1) * HD] for j in range(per_peer)]
            ready = prepare(heads, gcos, gsin)
            for j in range(per_peer):
                qs_ref[:, p * per_peer + j, :] = ready[j * rows : (j + 1) * rows]
        heads = [kv_ref[:, k * HD : (k + 1) * HD] for k in range(kv_count)]
        keys = prepare(heads, kcos_ref[...], ksin_ref[...]).astype(BF16)
        for k in range(kv_count):
            key = keys[k * rows : (k + 1) * rows]
            entry_ref[:, k * HD : (k + 1) * HD] = key
            es_ref[:, k, :] = key.astype(F32)
            value = kv_ref[:, width + k * HD : width + (k + 1) * HD]
            entry_ref[:, width + k * HD : width + (k + 1) * HD] = value
            es_ref[:, kv_count + k, :] = value.astype(F32)

    scale = HD ** (-0.5)
    heads = kv_count * group_size
    positions = lax.broadcasted_iota(jnp.int32, (heads, length_cap), 1)
    places = lax.broadcasted_iota(jnp.int32, (length_cap, 2 * width), 0)
    spans = [slice(k * group_size, (k + 1) * group_size) for k in range(kv_count)]
    first = step * rows_step
    blocks, scores, weights, results = [], [], [], []
    for i in range(rows_step):
        entry = es_ref[first + i]
        entry = jnp.concatenate(
            [entry[k : k + 1] for k in range(2 * kv_count)], axis=1
        ).astype(BF16)
        blocks.append(jnp.where(places == lens_ref[first + i], entry, cache_ref[i]))
    for i in range(rows_step):
        queries = qs_ref[first + i].astype(BF16)
        scores.append(
            jnp.concatenate(
                [
                    lax.dot_general(
                        queries[spans[k]], blocks[i][:, k * HD : (k + 1) * HD],
                        (((1,), (1,)), ((), ())), preferred_element_type=F32,
                    )
                    for k in range(kv_count)
                ],
                axis=0,
            )
        )
    for i in range(rows_step):
        score = jnp.where(positions <= lens_ref[first + i], scores[i] * scale, -1e30)
        peak = jnp.max(score, axis=1, keepdims=True)
        weights.append(jnp.exp(score - peak).astype(BF16))
    for i in range(rows_step):
        total = jnp.dot(weights[i], ones, preferred_element_type=F32)
        summed = jnp.concatenate(
            [
                jnp.dot(
                    weights[i][spans[k]],
                    blocks[i][:, width + k * HD : width + (k + 1) * HD],
                    preferred_element_type=F32,
                )
                for k in range(kv_count)
            ],
            axis=0,
        )
        results.append(summed / total)
    for i in range(rows_step):
        os_ref[first + i] = results[i]

    @pl.when(step == pl.num_programs(0) - 1)
    def _():
        for p in range(peers):
            for j in range(per_peer):
                att_ref[p, :, j * HD : (j + 1) * HD] = os_ref[:, p * per_peer + j, :].astype(BF16)


def attend(q_peers, q_width, kv_rows, cache_kv, lengths, q_gain, k_gain):
    peers, rows, sent_width = q_peers.shape
    length_cap, entry_width = cache_kv.shape[1:]
    kv_count = entry_width // (2 * HD)
    heads = peers * q_width // HD
    rows_step = 8
    half = HD // 2
    frequency = ROPE_BASE ** (-2.0 * jnp.arange(half, dtype=F32) / HD)
    angles = lengths.astype(F32)[:, None] * frequency[None, :]
    cosine = jnp.concatenate([jnp.cos(angles), jnp.cos(angles)], axis=-1)
    sine = jnp.concatenate([jnp.sin(angles), jnp.sin(angles)], axis=-1)
    turn = (jnp.eye(HD, k=half) - jnp.eye(HD, k=-half)).astype(BF16)
    tables = [
        table * gain[None, :]
        for gain in (q_gain, k_gain)
        for table, gain in ((cosine, gain), (sine, jnp.roll(gain, half)))
    ]
    whole = lambda shape: pl.BlockSpec(shape, lambda i, lens: (0,) * len(shape))
    return pl.pallas_call(
        functools.partial(
            attend_kernel, rows_step=rows_step, kv_count=kv_count, group_size=heads // kv_count
        ),
        grid_spec=pltpu.PrefetchScalarGridSpec(
            num_scalar_prefetch=1,
            grid=(rows // rows_step,),
            in_specs=[
                whole((peers, rows, sent_width)),
                whole((rows, entry_width)),
                whole((rows, HD)),
                whole((rows, HD)),
                whole((rows, HD)),
                whole((rows, HD)),
                whole((HD, HD)),
                pl.BlockSpec((rows_step, length_cap, entry_width), lambda i, lens: (i, 0, 0)),
            ],
            out_specs=[whole((peers, rows, q_width)), whole((rows, entry_width))],
            scratch_shapes=[
                pltpu.VMEM((rows, heads, HD), F32),
                pltpu.VMEM((rows, 2 * kv_count, HD), F32),
                pltpu.VMEM((rows, heads, HD), F32),
            ],
        ),
        out_shape=[
            jax.ShapeDtypeStruct((peers, rows, q_width), BF16),
            jax.ShapeDtypeStruct((rows, entry_width), BF16),
        ],
        compiler_params=pltpu.CompilerParams(vmem_limit_bytes=VMEM_BYTES),
        cost_estimate=pl.CostEstimate(
            flops=4 * rows * heads * HD * length_cap,
            bytes_accessed=cache_kv.size * 2 + q_peers.size * 4,
            transcendentals=rows * heads * length_cap,
        ),
        name="attend",
    )(lengths, q_peers, kv_rows, *tables, turn, cache_kv)


WINDOW = 16


def place_kernel(
    lens_ref, distance_ref, rank_ref, entry_ref, cache_ref, *refs,
):
    *landed_refs, out_ref, rows_ref, in_sems, out_sems = refs
    rows = out_ref.shape[0]

    def copy_in(row, source, source_row):
        return pltpu.make_async_copy(source.at[source_row], rows_ref.at[row], in_sems.at[row])

    def copy_out(row):
        return pltpu.make_async_copy(rows_ref.at[row], out_ref.at[row], out_sems.at[row])

    def begin(row, carry):
        @pl.when(distance_ref[row] == 0)
        def _():
            copy_in(row, cache_ref, row).start()

        for distance, landed_ref in enumerate(landed_refs, 1):

            @pl.when(distance_ref[row] == distance)
            def _(landed_ref=landed_ref):
                copy_in(row, landed_ref, rank_ref[row]).start()

        return carry

    def renew(row, carry):
        copy_in(row, cache_ref, row).wait()
        start = pl.multiple_of(lens_ref[row] // WINDOW * WINDOW, WINDOW)
        window = rows_ref.at[row, pl.ds(start, WINDOW)]
        position = lax.broadcasted_iota(jnp.int32, window.shape, 0) + start
        window[...] = jnp.where(position == lens_ref[row], entry_ref[row], window[...])
        copy_out(row).start()
        return carry

    def finish(row, carry):
        copy_out(row).wait()
        return carry

    lax.fori_loop(0, rows, begin, 0)
    lax.fori_loop(0, rows, renew, 0)
    lax.fori_loop(0, rows, finish, 0)


def place_cache(lengths, distance, rank, entries, cache_kv, landed):
    rows, length_cap, entry_width = cache_kv.shape
    return pl.pallas_call(
        place_kernel,
        grid_spec=pltpu.PrefetchScalarGridSpec(
            num_scalar_prefetch=3,
            grid=(1,),
            in_specs=[
                pl.BlockSpec((rows, 1, entry_width), lambda i, a, b, c: (0, 0, 0)),
            ]
            + [pl.BlockSpec(memory_space=pl.ANY)] * (1 + len(landed)),
            out_specs=pl.BlockSpec(memory_space=pl.ANY),
            scratch_shapes=[
                pltpu.VMEM((rows, length_cap, entry_width), BF16),
                pltpu.SemaphoreType.DMA((rows,)),
                pltpu.SemaphoreType.DMA((rows,)),
            ],
        ),
        out_shape=jax.ShapeDtypeStruct(cache_kv.shape, BF16),
        compiler_params=pltpu.CompilerParams(vmem_limit_bytes=VMEM_BYTES),
        cost_estimate=pl.CostEstimate(
            flops=0, bytes_accessed=cache_kv.size * 4, transcendentals=0
        ),
        name="place_cache",
    )(lengths, distance, rank, entries[:, None, :], cache_kv, *landed)


def pick_kernel(slot_ref, *refs):
    count = len(refs) // 2
    for source, target in zip(refs[:count], refs[count:]):
        target[...] = source[...]


def pick_caches(slots, cache_kv):
    shifts, count = slots.shape
    block = (1,) + cache_kv.shape[1:]
    return pl.pallas_call(
        pick_kernel,
        grid_spec=pltpu.PrefetchScalarGridSpec(
            num_scalar_prefetch=1,
            grid=(count,),
            in_specs=[
                pl.BlockSpec(block, lambda i, slots, k=k: (slots[k, i], 0, 0))
                for k in range(shifts)
            ],
            out_specs=[pl.BlockSpec(block, lambda i, slots: (i, 0, 0)) for k in range(shifts)],
        ),
        out_shape=[
            jax.ShapeDtypeStruct((count,) + cache_kv.shape[1:], BF16) for k in range(shifts)
        ],
        compiler_params=pltpu.CompilerParams(vmem_limit_bytes=VMEM_BYTES),
        cost_estimate=pl.CostEstimate(
            flops=0,
            bytes_accessed=4 * shifts * count * cache_kv.shape[1] * cache_kv.shape[2],
            transcendentals=0,
        ),
        name="pick_caches",
    )(slots, *([cache_kv] * shifts))


def exchange(array, groups=PLANES):
    return lax.all_to_all(array, "cuts", 0, 0, tiled=True, axis_index_groups=groups)


def behind(array, *marks):
    return lax.optimization_barrier((array, *marks))[0]


def swap_cores(array):
    return lax.ppermute(array, "inst", [(g, g ^ 1) for g in range(4)])


def rows_kernel(places_ref, *refs):
    *pieces, weights_ref, out_ref, rows_ref, total_ref = refs
    step = pl.program_id(0)
    at = 0
    for piece in pieces:
        count = piece.shape[0] * piece.shape[1]
        rows_ref[at : at + count] = piece[...].reshape(count, piece.shape[2])
        at += count
    part = jnp.dot(rows_ref[...], weights_ref[...], preferred_element_type=F32)

    @pl.when(step == 0)
    def _():
        total_ref[...] = part

    @pl.when(step > 0)
    def _():
        total_ref[...] += part

    @pl.when(step == pl.num_programs(0) - 1)
    def _():
        lines = out_ref.shape[1]
        for line in range(out_ref.shape[0]):
            out_ref[places_ref[line]] = total_ref[line * lines : (line + 1) * lines].astype(BF16)


def project_rows(places, pieces, weights):
    rows = sum(piece.shape[0] * piece.shape[1] for piece in pieces)
    width, columns = weights.shape
    depth = width // 4
    out = (SIDE, rows // SIDE, columns)
    return pl.pallas_call(
        rows_kernel,
        grid_spec=pltpu.PrefetchScalarGridSpec(
            num_scalar_prefetch=1,
            grid=(width // depth,),
            in_specs=[
                pl.BlockSpec(piece.shape[:2] + (depth,), lambda i, places: (0, 0, i))
                for piece in pieces
            ]
            + [pl.BlockSpec((depth, columns), lambda i, places: (i, 0))],
            out_specs=pl.BlockSpec(out, lambda i, places: (0, 0, 0)),
            scratch_shapes=[pltpu.VMEM((rows, depth), BF16), pltpu.VMEM((rows, columns), F32)],
        ),
        out_shape=jax.ShapeDtypeStruct(out, BF16),
        compiler_params=pltpu.CompilerParams(vmem_limit_bytes=VMEM_BYTES),
        cost_estimate=pl.CostEstimate(
            flops=2 * rows * width * columns,
            bytes_accessed=2 * (rows * width + weights.size),
            transcendentals=0,
        ),
        name="project_rows",
    )(places, *pieces, weights)


def out_kernel(heads_ref, *refs, spots):
    out_ref = refs[-1]
    sources, _, rows, _ = heads_ref.shape
    steps = pl.num_programs(0)

    def add_up(weights):
        total = 0.0
        for (offset, first), piece in zip(spots, weights):
            depth = piece.shape[0]
            heads = heads_ref[:, offset].reshape(sources * rows, -1)[:, first : first + depth]
            total += jnp.dot(heads, piece[...], preferred_element_type=F32)
        out_ref[...] = total.astype(BF16)

    @pl.when(pl.program_id(0) < steps // 2)
    def _():
        add_up(refs[: len(spots)])

    @pl.when(pl.program_id(0) >= steps // 2)
    def _():
        add_up(refs[len(spots) : 2 * len(spots)])


def project_out(heads, spots, mine, other):
    sources, _, rows, _ = heads.shape
    half = mine[0].shape[1]
    tile = 512
    steps = half // tile
    first = [
        pl.BlockSpec((part.shape[0], tile), lambda i: (0, jnp.minimum(i, steps - 1)))
        for part in mine
    ]
    second = [
        pl.BlockSpec((part.shape[0], tile), lambda i: (0, jnp.maximum(i - steps, 0)))
        for part in other
    ]
    return pl.pallas_call(
        functools.partial(out_kernel, spots=spots),
        grid=(2 * steps,),
        in_specs=[pl.BlockSpec(heads.shape, lambda i: (0, 0, 0, 0))] + first + second,
        out_specs=pl.BlockSpec((sources * rows, tile), lambda i: (0, i)),
        out_shape=jax.ShapeDtypeStruct((sources * rows, 2 * half), BF16),
        compiler_params=pltpu.CompilerParams(vmem_limit_bytes=VMEM_BYTES),
        cost_estimate=pl.CostEstimate(
            flops=2 * heads.size * 2 * half,
            bytes_accessed=4 * sum(part.size for part in mine),
            transcendentals=0,
        ),
        name="project_out",
    )(heads, *mine, *other)


def body(
    hidden,
    cache_kv,
    cache_len,
    mig_source,
    expert_ids,
    gate_w,
    attn_gain,
    w_query,
    w_keyval,
    q_gain,
    k_gain,
    w_out,
    moe_gain,
    w_gate,
    w_up,
    w_down,
):
    group_count = lax.axis_size("inst")
    cut_count = lax.axis_size("cuts")
    local_rows, width = hidden.shape
    group_total = local_rows * cut_count
    group_id = lax.axis_index("inst")
    cut_id = lax.axis_index("cuts")
    low = cut_id % 2 == 0
    at_x = (cut_id // 2) % SIDE
    at_y = cut_id // (2 * SIDE)
    slot_ids = jnp.arange(local_rows, dtype=jnp.int32)
    own_rows = (group_id * cut_count + cut_id) * local_rows + slot_ids

    normed = norm_rows(hidden.astype(F32), attn_gain.astype(F32)).astype(BF16)
    half_rows = local_rows // 2
    after, before = shift(normed, 0, SIDE - 1), shift(normed, 0, 1)
    across = jnp.concatenate(
        [shift(after[:half_rows], 0, SIDE - 1), shift(before[half_rows:], 0, 1)]
    )
    line = jnp.zeros((SIDE,) + normed.shape, BF16)
    for offset, rows in enumerate((normed, after, across, before)):
        line = lax.dynamic_update_slice(line, rows[None], ((at_x + offset) % SIDE, 0, 0))
    half_line = SIDE // 2
    after, before = shift(line, SIDE - 1, 0), shift(line, 1, 0)
    across = [shift(after[:half_line], SIDE - 1, 0), shift(before[half_line:], 1, 0)]

    facts = behind(jnp.stack([mig_source, cache_len]).astype(F32), line)
    all_facts = lax.all_to_all(
        jnp.broadcast_to(facts[None], (group_count,) + facts.shape), "inst", 0, 0, tiled=True
    )

    w_keyval_pair = from_pair(w_keyval, 0)
    first_core = group_id % 2 == 0
    half_depth = width // 2
    w_query_part = from_pair(
        lax.dynamic_slice_in_dim(w_query, (group_id % 2) * half_depth, half_depth, 0), 0
    )
    w_query_rest = swap_cores(w_query_part)

    half_width = width // 2
    w_mine = lax.dynamic_slice_in_dim(w_out, (group_id % 2) * half_width, half_width, 1)
    w_here = jnp.concatenate([w_mine, from_pair(w_mine, 1)])
    w_there = mirror(w_here)

    w_gate, w_up, w_here = lax.optimization_barrier((w_gate, w_up, w_here))
    one_pair = from_pair(jnp.where(first_core, w_gate, w_up), 1)
    w_down, w_query_rest = lax.optimization_barrier((w_down, w_query_rest))
    w_down_pair = from_pair(w_down, 0)

    w_query_pair = jnp.where(
        first_core,
        jnp.concatenate([w_query_part, w_query_rest]),
        jnp.concatenate([w_query_rest, w_query_part]),
    )
    w_project = lax.optimization_barrier(
        jnp.concatenate(
            [w_query, w_query_pair, behind(w_keyval, after), behind(w_keyval_pair, after)], axis=1
        )
    )
    q_width = 2 * w_query.shape[1]
    kv_width = w_keyval.shape[1]

    places = (at_y + jnp.arange(SIDE, dtype=jnp.int32)) % SIDE
    projected = project_rows(places, [line, after, *across, before], w_project)
    arrived = exchange(projected.reshape(PLANE, local_rows, -1))

    all_facts = behind(all_facts, projected)
    goes_to = all_facts[:, 0].astype(jnp.int32) == own_rows[None, :]
    lengths = jnp.sum(jnp.where(goes_to, all_facts[:, 1], 0.0), axis=0).astype(jnp.int32)
    targets = jnp.arange(group_count, dtype=jnp.int32)
    leaving = goes_to & (targets[:, None] != group_id)
    leave_rank = jnp.cumsum(leaving.astype(jnp.int32), axis=1) - 1
    chosen = leaving[:, None, :] & (
        leave_rank[:, None, :] == jnp.arange(MIG, dtype=jnp.int32)[None, :, None]
    )
    send_slot = jnp.sum(jnp.where(chosen, slot_ids[None, None, :], 0), axis=2)
    source_group = mig_source // group_total
    arriving = source_group != group_id
    from_group = (source_group[None, :] == targets[:, None]) & arriving[None, :]
    arrival_rank = jnp.sum(
        jnp.where(from_group, jnp.cumsum(from_group.astype(jnp.int32), axis=1) - 1, 0), axis=0
    )
    source_pick = jnp.where(arriving, source_group, 0)


    own_kv = arrived[:, :, q_width : q_width + kv_width]
    pair_kv = arrived[:, :, q_width + kv_width :]
    kv_rows = jnp.where(
        low,
        jnp.concatenate([own_kv, pair_kv], axis=2),
        jnp.concatenate([pair_kv, own_kv], axis=2),
    )
    kv_rows = jnp.transpose(kv_rows, (1, 0, 2)).reshape(local_rows, -1)
    attention, entries = attend(arrived, q_width, kv_rows, cache_kv, lengths, q_gain, k_gain)

    attention = attention.reshape(SIDE, 2, 2, local_rows, q_width)
    left = at_x < 2
    near = jnp.where(left, attention[:, 0], attention[:, 1])
    far = jnp.where(left, attention[:, 1], attention[:, 0])[:, ::-1]
    attention = jnp.stack([near, far], axis=2).reshape(2 * SIDE, 2, local_rows, q_width)
    heads = exchange(attention, BLOCKS)
    heads = behind(heads, w_down_pair)
    other_pair = swap_cores(behind(one_pair, heads))
    mine = [w_here, w_there]
    other = [swap_cores(behind(part, projected)) for part in mine]
    partial_value = project_out(heads, [(0, 0), (1, 0)], mine, other)
    sums = exchange(partial_value.reshape(2 * SIDE, local_rows, width), BLOCKS)

    sums = behind(sums, other_pair)

    attn_out = jnp.sum(sums.astype(F32), axis=0)
    mine_out, other_out = attn_out[:, :half_width], attn_out[:, half_width:]
    mixed_rows = hidden.astype(F32) + jnp.concatenate(
        [jnp.where(first_core, mine_out, other_out), jnp.where(first_core, other_out, mine_out)],
        axis=1,
    )
    rows_entries = jnp.concatenate([mixed_rows, entries.astype(F32)], axis=1)
    got_rows = lax.all_to_all(rows_entries[send_slot], "inst", 0, 0, tiled=True)
    rows_entries = jnp.where(
        arriving[:, None], got_rows[source_pick, arrival_rank], rows_entries
    )
    mixed_rows = rows_entries[:, :width]
    new_entries = rows_entries[:, width:].astype(BF16)

    shifts = jnp.arange(1, group_count, dtype=jnp.int32)
    picked = pick_caches(
        behind(send_slot, got_rows)[(group_id + shifts) % group_count], cache_kv
    )
    landed = [
        lax.ppermute(
            array, "inst", [(g, (g + distance) % group_count) for g in range(group_count)]
        )
        for distance, array in zip(range(1, group_count), picked)
    ]
    distance = (group_id - source_group) % group_count
    cache_next = place_cache(cache_len, distance, arrival_rank, new_entries, cache_kv, landed)

    moe_local = norm_rows(mixed_rows, moe_gain.astype(F32)).astype(BF16)

    expert_range = jnp.arange(PLANE, dtype=jnp.int32)
    combine = jnp.sum(
        jnp.where(
            expert_ids[:, :, None] == expert_range[None, None, :],
            gate_w.astype(F32)[:, :, None],
            0.0,
        ),
        axis=1,
    )
    flags = jnp.transpose(combine) > 0.0
    rank = jnp.cumsum(flags.astype(jnp.int32), axis=1) - 1
    slot_range = jnp.arange(MOST, dtype=jnp.int32)
    match = flags[:, None, :] & (rank[:, None, :] == slot_range[None, :, None])
    match = match.reshape(PLANE * MOST, local_rows)
    slab = jnp.dot(match.astype(BF16), moe_local, preferred_element_type=F32).astype(BF16)
    slab_rows = exchange(slab.reshape(PLANE, MOST, width)).reshape(PLANE * MOST, width)
    slab_rows = behind(slab_rows, *picked)

    def expert_half(gate_part, upward, down):
        activation = (jax.nn.silu(gate_part) * upward).astype(BF16)
        return jnp.dot(activation, down, preferred_element_type=F32)

    own_gate = jnp.dot(slab_rows, w_gate, preferred_element_type=F32)
    own_up = jnp.dot(slab_rows, w_up, preferred_element_type=F32)
    pair_one = jnp.dot(slab_rows, one_pair, preferred_element_type=F32)
    pair_other = jnp.dot(slab_rows, other_pair, preferred_element_type=F32)
    pair_gate = jnp.where(first_core, pair_one, pair_other)
    pair_up = jnp.where(first_core, pair_other, pair_one)
    expert_out = (
        expert_half(own_gate, own_up, w_down) + expert_half(pair_gate, pair_up, w_down_pair)
    ).astype(BF16)
    returned = exchange(expert_out.reshape(PLANE, MOST, width)).reshape(PLANE * MOST, width)
    returned = behind(returned, cache_next)
    slot_gate = jnp.where(
        match, jnp.repeat(jnp.transpose(combine), MOST, axis=0), 0.0
    ).astype(BF16)
    moe_out = lax.dot_general(
        slot_gate, returned, (((0,), (0,)), ((), ())), preferred_element_type=F32
    )
    hidden_next = (mixed_rows + moe_out).astype(BF16)
    return (hidden_next, cache_next)


def solution(mesh):
    in_specs = (
        P(("inst", "cuts"), None),
        P(("inst", "cuts"), None, None),
        P(("inst", "cuts")),
        P(("inst", "cuts")),
        P(("inst", "cuts"), None),
        P(("inst", "cuts"), None),
        P(),
        P(None, "cuts"),
        P(None, "cuts"),
        P(),
        P(),
        P("cuts", None),
        P(),
        P(None, "cuts"),
        P(None, "cuts"),
        P("cuts", None),
    )
    out_specs = (P(("inst", "cuts"), None), P(("inst", "cuts"), None, None))
    return jax.shard_map(body, mesh=mesh, in_specs=in_specs, out_specs=out_specs, check_vma=False)
```

```python
import functools
import jax
import jax.numpy as jnp
from jax import lax
from jax.experimental import pallas as pl
from jax.experimental.pallas import tpu as pltpu
from jax.sharding import PartitionSpec as P

HD = 128
MIG = 2
MOST = 4
EPSILON = 1e-06
ROPE_BASE = 1000000.0
SIDE = 4
PLANE = SIDE * SIDE
VMEM_BYTES = 56 * 1024 * 1024
BF16 = jnp.bfloat16
F32 = jnp.float32


def cut_index(y, x, z):
    return (y * SIDE + x) * 2 + z


PLANES = [[cut_index(y, x, z) for y in range(SIDE) for x in range(SIDE)] for z in range(2)]
BLOCKS = [
    [cut_index(y, x, z) for y in range(SIDE) for x in (first, first + 1)]
    for first in (0, 2)
    for z in range(2)
]


def shift(array, dy, dx):
    moves = [
        (cut_index(y, x, z), cut_index((y + dy) % SIDE, (x + dx) % SIDE, z))
        for y in range(SIDE)
        for x in range(SIDE)
        for z in range(2)
    ]
    return lax.ppermute(array, "cuts", moves)


def mirror(array):
    moves = [
        (cut_index(y, x, z), cut_index(y, SIDE - 1 - x, z))
        for y in range(SIDE)
        for x in range(SIDE)
        for z in range(2)
    ]
    return lax.ppermute(array, "cuts", moves)


def pair_perm(side):
    out = []
    for z in range(4):
        for core in range(2):
            way = (side + core) % 2
            other = z ^ 1 if way == 0 else (z + 1 if z % 2 else z - 1) % 4
            for y in range(SIDE):
                for x in range(SIDE):
                    out.append(
                        (
                            ((z // 2) * 2 + core) * 32 + cut_index(y, x, z % 2),
                            ((other // 2) * 2 + core) * 32 + cut_index(y, x, other % 2),
                        )
                    )
    return out


def from_pair(array, side):
    return lax.ppermute(array, ("inst", "cuts"), pair_perm(side))


def norm_rows(values, gain_vec):
    mean_square = jnp.mean(values * values, axis=-1, keepdims=True)
    return values * lax.rsqrt(mean_square + EPSILON) * gain_vec


def attend_kernel(
    lens_ref, q_ref, kv_ref, gcos_ref, gsin_ref, kcos_ref, ksin_ref, turn_ref, cache_ref,
    att_ref, entry_ref, qs_ref, es_ref, os_ref, *, rows_step, kv_count, group_size,
):
    step = pl.program_id(0)
    peers, rows = q_ref.shape[:2]
    per_peer = att_ref.shape[2] // HD
    length_cap = cache_ref.shape[1]
    width = kv_count * HD
    ones = jnp.ones((HD, HD), BF16)

    @pl.when(step == 0)
    def _():
        def prepare(heads, cosine, sine):
            stacked = jnp.concatenate(heads, axis=0)
            values = stacked.astype(F32)
            squares = values * values
            high = squares.astype(BF16)
            low = (squares - high.astype(F32)).astype(BF16)
            total = jnp.dot(high, ones, preferred_element_type=F32)
            total += jnp.dot(low, ones, preferred_element_type=F32)
            turned = jnp.dot(stacked, turn_ref[...], preferred_element_type=F32)
            inverse = lax.rsqrt(total * (1.0 / HD) + EPSILON)
            count = len(heads)
            cosine = jnp.concatenate([cosine] * count, axis=0)
            sine = jnp.concatenate([sine] * count, axis=0)
            return (values * cosine + turned * sine) * inverse

        gcos, gsin = gcos_ref[...], gsin_ref[...]
        for p in range(peers):
            heads = [q_ref[p, :, j * HD : (j + 1) * HD] for j in range(per_peer)]
            ready = prepare(heads, gcos, gsin)
            for j in range(per_peer):
                qs_ref[:, p * per_peer + j, :] = ready[j * rows : (j + 1) * rows]
        heads = [kv_ref[:, k * HD : (k + 1) * HD] for k in range(kv_count)]
        keys = prepare(heads, kcos_ref[...], ksin_ref[...]).astype(BF16)
        for k in range(kv_count):
            key = keys[k * rows : (k + 1) * rows]
            entry_ref[:, k * HD : (k + 1) * HD] = key
            es_ref[:, k, :] = key.astype(F32)
            value = kv_ref[:, width + k * HD : width + (k + 1) * HD]
            entry_ref[:, width + k * HD : width + (k + 1) * HD] = value
            es_ref[:, kv_count + k, :] = value.astype(F32)

    scale = HD ** (-0.5)
    heads = kv_count * group_size
    positions = lax.broadcasted_iota(jnp.int32, (heads, length_cap), 1)
    places = lax.broadcasted_iota(jnp.int32, (length_cap, 2 * width), 0)
    spans = [slice(k * group_size, (k + 1) * group_size) for k in range(kv_count)]
    first = step * rows_step
    blocks, scores, weights, results = [], [], [], []
    for i in range(rows_step):
        entry = es_ref[first + i]
        entry = jnp.concatenate(
            [entry[k : k + 1] for k in range(2 * kv_count)], axis=1
        ).astype(BF16)
        blocks.append(jnp.where(places == lens_ref[first + i], entry, cache_ref[i]))
    for i in range(rows_step):
        queries = qs_ref[first + i].astype(BF16)
        scores.append(
            jnp.concatenate(
                [
                    lax.dot_general(
                        queries[spans[k]], blocks[i][:, k * HD : (k + 1) * HD],
                        (((1,), (1,)), ((), ())), preferred_element_type=F32,
                    )
                    for k in range(kv_count)
                ],
                axis=0,
            )
        )
    for i in range(rows_step):
        score = jnp.where(positions <= lens_ref[first + i], scores[i] * scale, -1e30)
        peak = jnp.max(score, axis=1, keepdims=True)
        weights.append(jnp.exp(score - peak).astype(BF16))
    for i in range(rows_step):
        total = jnp.dot(weights[i], ones, preferred_element_type=F32)
        summed = jnp.concatenate(
            [
                jnp.dot(
                    weights[i][spans[k]],
                    blocks[i][:, width + k * HD : width + (k + 1) * HD],
                    preferred_element_type=F32,
                )
                for k in range(kv_count)
            ],
            axis=0,
        )
        results.append(summed / total)
    for i in range(rows_step):
        os_ref[first + i] = results[i]

    @pl.when(step == pl.num_programs(0) - 1)
    def _():
        for p in range(peers):
            for j in range(per_peer):
                att_ref[p, :, j * HD : (j + 1) * HD] = os_ref[:, p * per_peer + j, :].astype(BF16)


def attend(q_peers, q_width, kv_rows, cache_kv, lengths, q_gain, k_gain):
    peers, rows, sent_width = q_peers.shape
    length_cap, entry_width = cache_kv.shape[1:]
    kv_count = entry_width // (2 * HD)
    heads = peers * q_width // HD
    rows_step = 16
    half = HD // 2
    frequency = ROPE_BASE ** (-2.0 * jnp.arange(half, dtype=F32) / HD)
    angles = lengths.astype(F32)[:, None] * frequency[None, :]
    cosine = jnp.concatenate([jnp.cos(angles), jnp.cos(angles)], axis=-1)
    sine = jnp.concatenate([jnp.sin(angles), jnp.sin(angles)], axis=-1)
    turn = (jnp.eye(HD, k=half) - jnp.eye(HD, k=-half)).astype(BF16)
    tables = [
        table * gain[None, :]
        for gain in (q_gain, k_gain)
        for table, gain in ((cosine, gain), (sine, jnp.roll(gain, half)))
    ]
    whole = lambda shape: pl.BlockSpec(shape, lambda i, lens: (0,) * len(shape))
    return pl.pallas_call(
        functools.partial(
            attend_kernel, rows_step=rows_step, kv_count=kv_count, group_size=heads // kv_count
        ),
        grid_spec=pltpu.PrefetchScalarGridSpec(
            num_scalar_prefetch=1,
            grid=(rows // rows_step,),
            in_specs=[
                whole((peers, rows, sent_width)),
                whole((rows, entry_width)),
                whole((rows, HD)),
                whole((rows, HD)),
                whole((rows, HD)),
                whole((rows, HD)),
                whole((HD, HD)),
                pl.BlockSpec((rows_step, length_cap, entry_width), lambda i, lens: (i, 0, 0)),
            ],
            out_specs=[whole((peers, rows, q_width)), whole((rows, entry_width))],
            scratch_shapes=[
                pltpu.VMEM((rows, heads, HD), F32),
                pltpu.VMEM((rows, 2 * kv_count, HD), F32),
                pltpu.VMEM((rows, heads, HD), F32),
            ],
        ),
        out_shape=[
            jax.ShapeDtypeStruct((peers, rows, q_width), BF16),
            jax.ShapeDtypeStruct((rows, entry_width), BF16),
        ],
        compiler_params=pltpu.CompilerParams(vmem_limit_bytes=VMEM_BYTES),
        cost_estimate=pl.CostEstimate(
            flops=4 * rows * heads * HD * length_cap,
            bytes_accessed=cache_kv.size * 2 + q_peers.size * 4,
            transcendentals=rows * heads * length_cap,
        ),
        name="attend",
    )(lengths, q_peers, kv_rows, *tables, turn, cache_kv)


WINDOW = 16


def place_kernel(
    lens_ref, distance_ref, rank_ref, entry_ref, cache_ref, *refs,
):
    *landed_refs, out_ref, rows_ref, in_sems, out_sems = refs
    rows = out_ref.shape[0]

    def copy_in(row, source, source_row):
        return pltpu.make_async_copy(source.at[source_row], rows_ref.at[row], in_sems.at[row])

    def copy_out(row):
        return pltpu.make_async_copy(rows_ref.at[row], out_ref.at[row], out_sems.at[row])

    def begin(row, carry):
        @pl.when(distance_ref[row] == 0)
        def _():
            copy_in(row, cache_ref, row).start()

        for distance, landed_ref in enumerate(landed_refs, 1):

            @pl.when(distance_ref[row] == distance)
            def _(landed_ref=landed_ref):
                copy_in(row, landed_ref, rank_ref[row]).start()

        return carry

    def renew(row, carry):
        copy_in(row, cache_ref, row).wait()
        start = pl.multiple_of(lens_ref[row] // WINDOW * WINDOW, WINDOW)
        window = rows_ref.at[row, pl.ds(start, WINDOW)]
        position = lax.broadcasted_iota(jnp.int32, window.shape, 0) + start
        window[...] = jnp.where(position == lens_ref[row], entry_ref[row], window[...])
        copy_out(row).start()
        return carry

    def finish(row, carry):
        copy_out(row).wait()
        return carry

    lax.fori_loop(0, rows, begin, 0)
    lax.fori_loop(0, rows, renew, 0)
    lax.fori_loop(0, rows, finish, 0)


def place_cache(lengths, distance, rank, entries, cache_kv, landed):
    rows, length_cap, entry_width = cache_kv.shape
    return pl.pallas_call(
        place_kernel,
        grid_spec=pltpu.PrefetchScalarGridSpec(
            num_scalar_prefetch=3,
            grid=(1,),
            in_specs=[
                pl.BlockSpec((rows, 1, entry_width), lambda i, a, b, c: (0, 0, 0)),
            ]
            + [pl.BlockSpec(memory_space=pl.ANY)] * (1 + len(landed)),
            out_specs=pl.BlockSpec(memory_space=pl.ANY),
            scratch_shapes=[
                pltpu.VMEM((rows, length_cap, entry_width), BF16),
                pltpu.SemaphoreType.DMA((rows,)),
                pltpu.SemaphoreType.DMA((rows,)),
            ],
        ),
        out_shape=jax.ShapeDtypeStruct(cache_kv.shape, BF16),
        compiler_params=pltpu.CompilerParams(vmem_limit_bytes=VMEM_BYTES),
        cost_estimate=pl.CostEstimate(
            flops=0, bytes_accessed=cache_kv.size * 4, transcendentals=0
        ),
        name="place_cache",
    )(lengths, distance, rank, entries[:, None, :], cache_kv, *landed)


def pick_kernel(slot_ref, *refs):
    count = len(refs) // 2
    for source, target in zip(refs[:count], refs[count:]):
        target[...] = source[...]


def pick_caches(slots, cache_kv):
    shifts, count = slots.shape
    block = (1,) + cache_kv.shape[1:]
    return pl.pallas_call(
        pick_kernel,
        grid_spec=pltpu.PrefetchScalarGridSpec(
            num_scalar_prefetch=1,
            grid=(count,),
            in_specs=[
                pl.BlockSpec(block, lambda i, slots, k=k: (slots[k, i], 0, 0))
                for k in range(shifts)
            ],
            out_specs=[pl.BlockSpec(block, lambda i, slots: (i, 0, 0)) for k in range(shifts)],
        ),
        out_shape=[
            jax.ShapeDtypeStruct((count,) + cache_kv.shape[1:], BF16) for k in range(shifts)
        ],
        compiler_params=pltpu.CompilerParams(vmem_limit_bytes=VMEM_BYTES),
        cost_estimate=pl.CostEstimate(
            flops=0,
            bytes_accessed=4 * shifts * count * cache_kv.shape[1] * cache_kv.shape[2],
            transcendentals=0,
        ),
        name="pick_caches",
    )(slots, *([cache_kv] * shifts))


def exchange(array, groups=PLANES):
    return lax.all_to_all(array, "cuts", 0, 0, tiled=True, axis_index_groups=groups)


def behind(array, *marks):
    return lax.optimization_barrier((array, *marks))[0]


def swap_cores(array):
    return lax.ppermute(array, "inst", [(g, g ^ 1) for g in range(4)])


def rows_kernel(places_ref, *refs):
    *pieces, weights_ref, out_ref, rows_ref, total_ref = refs
    step = pl.program_id(0)
    at = 0
    for piece in pieces:
        count = piece.shape[0] * piece.shape[1]
        rows_ref[at : at + count] = piece[...].reshape(count, piece.shape[2])
        at += count
    part = jnp.dot(rows_ref[...], weights_ref[...], preferred_element_type=F32)

    @pl.when(step == 0)
    def _():
        total_ref[...] = part

    @pl.when(step > 0)
    def _():
        total_ref[...] += part

    @pl.when(step == pl.num_programs(0) - 1)
    def _():
        lines = out_ref.shape[1]
        for line in range(out_ref.shape[0]):
            out_ref[places_ref[line]] = total_ref[line * lines : (line + 1) * lines].astype(BF16)


def project_rows(places, pieces, weights):
    rows = sum(piece.shape[0] * piece.shape[1] for piece in pieces)
    width, columns = weights.shape
    depth = width // 4
    out = (SIDE, rows // SIDE, columns)
    return pl.pallas_call(
        rows_kernel,
        grid_spec=pltpu.PrefetchScalarGridSpec(
            num_scalar_prefetch=1,
            grid=(width // depth,),
            in_specs=[
                pl.BlockSpec(piece.shape[:2] + (depth,), lambda i, places: (0, 0, i))
                for piece in pieces
            ]
            + [pl.BlockSpec((depth, columns), lambda i, places: (i, 0))],
            out_specs=pl.BlockSpec(out, lambda i, places: (0, 0, 0)),
            scratch_shapes=[pltpu.VMEM((rows, depth), BF16), pltpu.VMEM((rows, columns), F32)],
        ),
        out_shape=jax.ShapeDtypeStruct(out, BF16),
        compiler_params=pltpu.CompilerParams(vmem_limit_bytes=VMEM_BYTES),
        cost_estimate=pl.CostEstimate(
            flops=2 * rows * width * columns,
            bytes_accessed=2 * (rows * width + weights.size),
            transcendentals=0,
        ),
        name="project_rows",
    )(places, *pieces, weights)


def out_kernel(heads_ref, *refs, spots):
    out_ref = refs[-1]
    sources, _, rows, _ = heads_ref.shape
    steps = pl.num_programs(0)

    def add_up(weights):
        total = 0.0
        for (offset, first), piece in zip(spots, weights):
            depth = piece.shape[0]
            heads = heads_ref[:, offset].reshape(sources * rows, -1)[:, first : first + depth]
            total += jnp.dot(heads, piece[...], preferred_element_type=F32)
        out_ref[...] = total.astype(BF16)

    @pl.when(pl.program_id(0) < steps // 2)
    def _():
        add_up(refs[: len(spots)])

    @pl.when(pl.program_id(0) >= steps // 2)
    def _():
        add_up(refs[len(spots) : 2 * len(spots)])


def project_out(heads, spots, mine, other):
    sources, _, rows, _ = heads.shape
    half = mine[0].shape[1]
    tile = 512
    steps = half // tile
    first = [
        pl.BlockSpec((part.shape[0], tile), lambda i: (0, jnp.minimum(i, steps - 1)))
        for part in mine
    ]
    second = [
        pl.BlockSpec((part.shape[0], tile), lambda i: (0, jnp.maximum(i - steps, 0)))
        for part in other
    ]
    return pl.pallas_call(
        functools.partial(out_kernel, spots=spots),
        grid=(2 * steps,),
        in_specs=[pl.BlockSpec(heads.shape, lambda i: (0, 0, 0, 0))] + first + second,
        out_specs=pl.BlockSpec((sources * rows, tile), lambda i: (0, i)),
        out_shape=jax.ShapeDtypeStruct((sources * rows, 2 * half), BF16),
        compiler_params=pltpu.CompilerParams(vmem_limit_bytes=VMEM_BYTES),
        cost_estimate=pl.CostEstimate(
            flops=2 * heads.size * 2 * half,
            bytes_accessed=4 * sum(part.size for part in mine),
            transcendentals=0,
        ),
        name="project_out",
    )(heads, *mine, *other)


def body(
    hidden,
    cache_kv,
    cache_len,
    mig_source,
    expert_ids,
    gate_w,
    attn_gain,
    w_query,
    w_keyval,
    q_gain,
    k_gain,
    w_out,
    moe_gain,
    w_gate,
    w_up,
    w_down,
):
    group_count = lax.axis_size("inst")
    cut_count = lax.axis_size("cuts")
    local_rows, width = hidden.shape
    group_total = local_rows * cut_count
    group_id = lax.axis_index("inst")
    cut_id = lax.axis_index("cuts")
    low = cut_id % 2 == 0
    at_x = (cut_id // 2) % SIDE
    at_y = cut_id // (2 * SIDE)
    slot_ids = jnp.arange(local_rows, dtype=jnp.int32)
    own_rows = (group_id * cut_count + cut_id) * local_rows + slot_ids

    normed = norm_rows(hidden.astype(F32), attn_gain.astype(F32)).astype(BF16)
    half_rows = local_rows // 2
    after, before = shift(normed, 0, SIDE - 1), shift(normed, 0, 1)
    across = jnp.concatenate(
        [shift(after[:half_rows], 0, SIDE - 1), shift(before[half_rows:], 0, 1)]
    )
    line = jnp.zeros((SIDE,) + normed.shape, BF16)
    for offset, rows in enumerate((normed, after, across, before)):
        line = lax.dynamic_update_slice(line, rows[None], ((at_x + offset) % SIDE, 0, 0))
    half_line = SIDE // 2
    after, before = shift(line, SIDE - 1, 0), shift(line, 1, 0)
    across = [shift(after[:half_line], SIDE - 1, 0), shift(before[half_line:], 1, 0)]

    facts = behind(jnp.stack([mig_source, cache_len]).astype(F32), line)
    all_facts = lax.all_to_all(
        jnp.broadcast_to(facts[None], (group_count,) + facts.shape), "inst", 0, 0, tiled=True
    )

    w_keyval_pair = from_pair(w_keyval, 0)
    first_core = group_id % 2 == 0
    half_depth = width // 2
    w_query_part = from_pair(
        lax.dynamic_slice_in_dim(w_query, (group_id % 2) * half_depth, half_depth, 0), 0
    )
    w_query_rest = swap_cores(w_query_part)

    half_width = width // 2
    w_mine = lax.dynamic_slice_in_dim(w_out, (group_id % 2) * half_width, half_width, 1)
    w_here = jnp.concatenate([w_mine, from_pair(w_mine, 1)])
    w_there = mirror(w_here)

    w_gate, w_up, w_here = lax.optimization_barrier((w_gate, w_up, w_here))
    one_pair = from_pair(jnp.where(first_core, w_gate, w_up), 1)
    w_down, w_query_rest = lax.optimization_barrier((w_down, w_query_rest))
    w_down_pair = from_pair(w_down, 0)

    w_query_pair = jnp.where(
        first_core,
        jnp.concatenate([w_query_part, w_query_rest]),
        jnp.concatenate([w_query_rest, w_query_part]),
    )
    w_project = lax.optimization_barrier(
        jnp.concatenate(
            [w_query, w_query_pair, behind(w_keyval, after), behind(w_keyval_pair, after)], axis=1
        )
    )
    q_width = 2 * w_query.shape[1]
    kv_width = w_keyval.shape[1]

    places = (at_y + jnp.arange(SIDE, dtype=jnp.int32)) % SIDE
    projected = project_rows(places, [line, after, *across, before], w_project)
    arrived = exchange(projected.reshape(PLANE, local_rows, -1))

    all_facts = behind(all_facts, projected)
    goes_to = all_facts[:, 0].astype(jnp.int32) == own_rows[None, :]
    lengths = jnp.sum(jnp.where(goes_to, all_facts[:, 1], 0.0), axis=0).astype(jnp.int32)
    targets = jnp.arange(group_count, dtype=jnp.int32)
    leaving = goes_to & (targets[:, None] != group_id)
    leave_rank = jnp.cumsum(leaving.astype(jnp.int32), axis=1) - 1
    chosen = leaving[:, None, :] & (
        leave_rank[:, None, :] == jnp.arange(MIG, dtype=jnp.int32)[None, :, None]
    )
    send_slot = jnp.sum(jnp.where(chosen, slot_ids[None, None, :], 0), axis=2)
    source_group = mig_source // group_total
    arriving = source_group != group_id
    from_group = (source_group[None, :] == targets[:, None]) & arriving[None, :]
    arrival_rank = jnp.sum(
        jnp.where(from_group, jnp.cumsum(from_group.astype(jnp.int32), axis=1) - 1, 0), axis=0
    )
    source_pick = jnp.where(arriving, source_group, 0)


    own_kv = arrived[:, :, q_width : q_width + kv_width]
    pair_kv = arrived[:, :, q_width + kv_width :]
    kv_rows = jnp.where(
        low,
        jnp.concatenate([own_kv, pair_kv], axis=2),
        jnp.concatenate([pair_kv, own_kv], axis=2),
    )
    kv_rows = jnp.transpose(kv_rows, (1, 0, 2)).reshape(local_rows, -1)
    attention, entries = attend(arrived, q_width, kv_rows, cache_kv, lengths, q_gain, k_gain)

    attention = attention.reshape(SIDE, 2, 2, local_rows, q_width)
    left = at_x < 2
    near = jnp.where(left, attention[:, 0], attention[:, 1])
    far = jnp.where(left, attention[:, 1], attention[:, 0])[:, ::-1]
    attention = jnp.stack([near, far], axis=2).reshape(2 * SIDE, 2, local_rows, q_width)
    heads = exchange(attention, BLOCKS)
    heads = behind(heads, w_down_pair)
    other_pair = swap_cores(behind(one_pair, heads))
    mine = [w_here, w_there]
    other = [swap_cores(behind(part, projected)) for part in mine]
    partial_value = project_out(heads, [(0, 0), (1, 0)], mine, other)
    sums = exchange(partial_value.reshape(2 * SIDE, local_rows, width), BLOCKS)

    sums = behind(sums, other_pair)

    attn_out = jnp.sum(sums.astype(F32), axis=0)
    mine_out, other_out = attn_out[:, :half_width], attn_out[:, half_width:]
    mixed_rows = hidden.astype(F32) + jnp.concatenate(
        [jnp.where(first_core, mine_out, other_out), jnp.where(first_core, other_out, mine_out)],
        axis=1,
    )
    rows_entries = jnp.concatenate([mixed_rows, entries.astype(F32)], axis=1)
    got_rows = lax.all_to_all(rows_entries[send_slot], "inst", 0, 0, tiled=True)
    rows_entries = jnp.where(
        arriving[:, None], got_rows[source_pick, arrival_rank], rows_entries
    )
    mixed_rows = rows_entries[:, :width]
    new_entries = rows_entries[:, width:].astype(BF16)

    shifts = jnp.arange(1, group_count, dtype=jnp.int32)
    picked = pick_caches(
        behind(send_slot, got_rows)[(group_id + shifts) % group_count], cache_kv
    )
    landed = [
        lax.ppermute(
            array, "inst", [(g, (g + distance) % group_count) for g in range(group_count)]
        )
        for distance, array in zip(range(1, group_count), picked)
    ]
    distance = (group_id - source_group) % group_count
    cache_next = place_cache(cache_len, distance, arrival_rank, new_entries, cache_kv, landed)

    moe_local = norm_rows(mixed_rows, moe_gain.astype(F32)).astype(BF16)

    expert_range = jnp.arange(PLANE, dtype=jnp.int32)
    combine = jnp.sum(
        jnp.where(
            expert_ids[:, :, None] == expert_range[None, None, :],
            gate_w.astype(F32)[:, :, None],
            0.0,
        ),
        axis=1,
    )
    flags = jnp.transpose(combine) > 0.0
    rank = jnp.cumsum(flags.astype(jnp.int32), axis=1) - 1
    slot_range = jnp.arange(MOST, dtype=jnp.int32)
    match = flags[:, None, :] & (rank[:, None, :] == slot_range[None, :, None])
    match = match.reshape(PLANE * MOST, local_rows)
    slab = jnp.dot(match.astype(BF16), moe_local, preferred_element_type=F32).astype(BF16)
    slab_rows = exchange(slab.reshape(PLANE, MOST, width)).reshape(PLANE * MOST, width)
    slab_rows = behind(slab_rows, *picked)

    def expert_half(gate_part, upward, down):
        activation = (jax.nn.silu(gate_part) * upward).astype(BF16)
        return jnp.dot(activation, down, preferred_element_type=F32)

    own_gate = jnp.dot(slab_rows, w_gate, preferred_element_type=F32)
    own_up = jnp.dot(slab_rows, w_up, preferred_element_type=F32)
    pair_one = jnp.dot(slab_rows, one_pair, preferred_element_type=F32)
    pair_other = jnp.dot(slab_rows, other_pair, preferred_element_type=F32)
    pair_gate = jnp.where(first_core, pair_one, pair_other)
    pair_up = jnp.where(first_core, pair_other, pair_one)
    expert_out = (
        expert_half(own_gate, own_up, w_down) + expert_half(pair_gate, pair_up, w_down_pair)
    ).astype(BF16)
    returned = exchange(expert_out.reshape(PLANE, MOST, width)).reshape(PLANE * MOST, width)
    returned = behind(returned, cache_next)
    slot_gate = jnp.where(
        match, jnp.repeat(jnp.transpose(combine), MOST, axis=0), 0.0
    ).astype(BF16)
    moe_out = lax.dot_general(
        slot_gate, returned, (((0,), (0,)), ((), ())), preferred_element_type=F32
    )
    hidden_next = (mixed_rows + moe_out).astype(BF16)
    return (hidden_next, cache_next)


def solution(mesh):
    in_specs = (
        P(("inst", "cuts"), None),
        P(("inst", "cuts"), None, None),
        P(("inst", "cuts")),
        P(("inst", "cuts")),
        P(("inst", "cuts"), None),
        P(("inst", "cuts"), None),
        P(),
        P(None, "cuts"),
        P(None, "cuts"),
        P(),
        P(),
        P("cuts", None),
        P(),
        P(None, "cuts"),
        P(None, "cuts"),
        P("cuts", None),
    )
    out_specs = (P(("inst", "cuts"), None), P(("inst", "cuts"), None, None))
    return jax.shard_map(body, mesh=mesh, in_specs=in_specs, out_specs=out_specs, check_vma=False)
```
